32 devices in a mesh: row: 4 (over y, x), vec: 8 (over z, core).
Axes of the slice: x: 2, y: 2, z: 4, core: 2. Of those that a mesh axis runs over, the one named last changes fastest.
Arguments:
- filtered: bfloat16 [32768, 2048], P(('row', 'vec')), may hold values from -6 to 6
- ritz: bfloat16 [2048, 1024], P('row', 'vec'), may hold values from -0.125 to 0.125
- panel_cols: float32 [32768, 512], P(('row', 'vec')), may hold values from -0.25 to 0.25
- panel_inverse: float32 [2, 256, 256], replicated, may hold values from -0.15 to 2, as said below
Outputs:
- eigvecs: float32 [32768, 1024], P('row', 'vec')
The draws below stay inside these ranges and needn't reach their ends.
Inputs may be any that keep to these rules, and one draw needn't show every extreme that they name: `panel_inverse`: each of the two blocks is upper triangular with a positive diagonal.
All inputs are finite; a program needn't handle non-finite values.
Results may differ from the reference program's by a relative error of at most 0.0003.
Values may be sent and summed in bfloat16 or wider, within the bound.
No kernel may reach another device: no remote copies, remote signals or barrier semaphores. Data moves between devices by JAX's collectives and lax.ppermute only.
A program may use at most 64 MiB of HBM per device.

```python
import math
import jax
import jax.numpy as jnp
from jax import lax

FILT = 2048
EIGS = 1024
PANEL = 256
ORDER = 32768


def draw_panel_inverse(key, part):
    key_diag = jax.random.fold_in(key, 11)
    key_off = jax.random.fold_in(key, 23)
    diag = jnp.exp(jax.random.uniform(key_diag, (2, PANEL), jnp.float32, math.log(0.5), math.log(2.0)))
    off = jax.random.uniform(key_off, (2, PANEL, PANEL), jnp.float32, -0.1, 0.1)
    upper = jnp.triu(off, 1)
    return upper + diag[:, :, None] * jnp.eye(PANEL, dtype=jnp.float32)[None, :, :]


def block_scale(own_key, extent, pieces, least, high):
    gain, own = 1.0, jax.random.fold_in(own_key, 6)
    for dim, parts in pieces:
        steps = jnp.exp(jax.random.uniform(jax.random.fold_in(own, dim), (parts,), jnp.float32, least / len(pieces), high / len(pieces)))
        gain = gain * jnp.repeat(steps, extent[dim] // parts).reshape([-1 if axis == dim else 1 for axis in range(len(extent))])
    return gain


def noise(stream_key, extent, deviation, most, cuts=(), held_as=jnp.bfloat16):
    loudness = block_scale(stream_key, extent, cuts, -0.22, 0.18) if cuts else 1.0
    values = jax.random.normal(stream_key, extent, jnp.float32) * deviation * loudness
    return jnp.minimum(jnp.maximum(values, -most), most).astype(held_as)


def setup_inputs(seed: int = 0) -> dict:
    key_of = jax.random.split(jax.random.key(seed), 5)
    filtered = noise(key_of[0], (ORDER, FILT), 1.0, 6.0, ((0, 32),))
    ritz = noise(key_of[1], (FILT, EIGS), FILT ** -0.5, 0.125, ((0, 4), (1, 8)))
    panel_cols = noise(key_of[2], (ORDER, 2 * PANEL), (2 * PANEL) ** -0.5, 0.25, ((0, 32),), jnp.float32)
    panel_inverse = draw_panel_inverse(jax.random.fold_in(key_of[4], 71), 0)
    return dict(filtered=filtered, ritz=ritz, panel_cols=panel_cols, panel_inverse=panel_inverse)


def reference(filtered, ritz, panel_cols, panel_inverse):
    highest = lax.Precision.HIGHEST
    rotated = jnp.dot(filtered, ritz, preferred_element_type=jnp.float32)
    total = rotated.shape[0]
    last_x = jnp.dot(panel_inverse[1], rotated[total - PANEL:], precision=highest)
    middle = rotated[total - 2 * PANEL:total - PANEL] - jnp.dot(panel_cols[total - 2 * PANEL:total - PANEL, PANEL:], last_x, precision=highest)
    next_x = jnp.dot(panel_inverse[0], middle, precision=highest)
    rest = rotated[:total - 2 * PANEL] - jnp.dot(panel_cols[:total - 2 * PANEL, :PANEL], next_x, precision=highest)
    rest = rest - jnp.dot(panel_cols[:total - 2 * PANEL, PANEL:], last_x, precision=highest)
    return jnp.concatenate([rest, next_x, last_x], axis=0)
```

```python
import functools

import jax
import jax.numpy as jnp
from jax import lax
from jax.experimental import pallas as pl
from jax.experimental.pallas import tpu as pltpu
from jax.sharding import PartitionSpec as P

ROW, VEC = "row", "vec"


def swapped(value, axis, offset):
    return lax.ppermute(value, axis, [(i, i ^ offset) for i in range(lax.axis_size(axis))])


def split(value):
    high = value.astype(jnp.bfloat16)
    return high, (value - high.astype(jnp.float32)).astype(jnp.bfloat16)


def split_array(value):
    high = lax.reduce_precision(value, 8, 7)
    return high.astype(jnp.bfloat16), (value - high).astype(jnp.bfloat16)


def mul(a, b):
    return jnp.dot(a, b, preferred_element_type=jnp.float32)


def mul3(a, b):
    return mul(a[0], b[0]) + (mul(a[0], b[1]) + mul(a[1], b[0]))


def columns_kernel(
    width, depth,
    flags, filtered, cols_high, cols_low, tail_own, tail_other, cross, inverse, even, odd,
    out, power, solved, solved_high, solved_low, scale,
):
    step = pl.program_id(0)
    tile, half = out.shape[0], even.shape[1]

    @pl.when(step == 0)
    def _():
        own = pl.multiple_of(flags[1] * width, width)
        other = pl.multiple_of((1 - flags[1]) * width, width)
        for piece, ritz in enumerate((even, odd)):
            where = pl.ds(piece * half, half)
            solved[pl.ds(own, width), where] = mul(tail_own[...], ritz[...])
            solved[pl.ds(other, width), where] = mul(tail_other[...], ritz[...])
        last = mul3(split(inverse[1]), split(solved[width:, :]))
        middle = solved[:width, :] - mul3((cross[0], cross[1]), split(last))
        solved[width:, :] = last
        solved[:width, :] = mul3(split(inverse[0]), split(middle))
        high, low = split(solved[...])
        solved_high[...] = high
        solved_low[...] = low
        peak = jnp.concatenate(
            [jnp.max(jnp.abs(ritz[...].astype(jnp.float32)), axis=0, keepdims=True) for ritz in (even, odd)], axis=1
        )
        bound = 8.0 * depth * peak + 2.0 * width * jnp.max(jnp.abs(solved[...]), axis=0, keepdims=True)
        exponent = 14.0 - jnp.floor(jnp.log2(jnp.maximum(bound, 1e-30)))
        scale[...] = jnp.broadcast_to(jnp.exp2(exponent), scale.shape)
        power[...] = jnp.broadcast_to(jnp.exp2(-exponent), power.shape)

    for piece, ritz in enumerate((even, odd)):
        where = pl.ds(piece * half, half)
        total = mul(filtered[...], ritz[...])
        total -= mul(cols_high[...], solved_high[:, where])
        total -= mul(cols_high[...], solved_low[:, where]) + mul(cols_low[...], solved_high[:, where])
        out[:, where] = total * scale[0:1, where]

    @pl.when((flags[0] == 1) & (step >= pl.num_programs(0) - 2 * width // tile))
    def _():
        first = (step - (pl.num_programs(0) - 2 * width // tile)) * tile
        out[...] = solved[pl.ds(pl.multiple_of(first, tile), tile), :] * scale[0:1, :]


def columns(flags, filtered, cols, tails, cross, inverse, even, odd):
    rows, depth = filtered.shape
    width = inverse.shape[1]
    count = even.shape[1] + odd.shape[1]
    tile = 256
    whole = lambda a: pl.BlockSpec(a.shape, lambda i, f: (0,) * a.ndim)
    tiled = lambda a: pl.BlockSpec((tile, a.shape[1]), lambda i, f: (i, 0))
    return pl.pallas_call(
        functools.partial(columns_kernel, width, depth),
        grid_spec=pltpu.PrefetchScalarGridSpec(
            num_scalar_prefetch=1,
            grid=(rows // tile,),
            in_specs=[tiled(filtered), tiled(cols[0]), tiled(cols[1])]
            + [whole(a) for a in (tails[0], tails[1], cross, inverse, even, odd)],
            out_specs=[pl.BlockSpec((tile, count), lambda i, f: (i, 0)), pl.BlockSpec((8, count), lambda i, f: (0, 0))],
            scratch_shapes=[
                pltpu.VMEM((2 * width, count), jnp.float32),
                pltpu.VMEM((2 * width, count), jnp.bfloat16),
                pltpu.VMEM((2 * width, count), jnp.bfloat16),
                pltpu.VMEM((8, count), jnp.float32),
            ],
        ),
        out_shape=[jax.ShapeDtypeStruct((rows, count), jnp.float32), jax.ShapeDtypeStruct((8, count), jnp.float32)],
        compiler_params=pltpu.CompilerParams(vmem_limit_bytes=40 * 1024 * 1024),
        cost_estimate=pl.CostEstimate(
            flops=2 * (rows + 2 * width) * (depth + 6 * width) * count,
            bytes_accessed=filtered.nbytes * 2 + 4 * rows * count,
            transcendentals=0,
        ),
    )(flags, filtered, cols[0], cols[1], tails[0], tails[1], cross, inverse, even, odd)


def on_device(filtered, ritz, panel_cols, panel_inverse):
    rows, depth = filtered.shape
    width = panel_inverse.shape[1]
    n_row, n_vec = lax.axis_size(ROW), lax.axis_size(VEC)
    row, vec = lax.axis_index(ROW), lax.axis_index(VEC)
    core = vec % 2
    block, own_cols = ritz.shape
    is_last = (row == n_row - 1) & (vec == n_vec - 1)
    last = n_row * n_vec - 1
    lower = rows - 2 * width

    cross = jnp.concatenate(split_array(panel_cols[lower : lower + width, width:]), axis=0).reshape(-1, block)
    cross_rows = cross.shape[0] // n_row
    def part_of(r):
        return jnp.concatenate(
            [filtered[lower:, r * block : (r + 1) * block], cross[r * cross_rows : (r + 1) * cross_rows]], axis=0
        )
    part = jnp.where(is_last, part_of(n_row - 1), jnp.zeros((), filtered.dtype))
    for r in range(n_row - 1):
        part += lax.ppermute(part_of(r), (ROW, VEC), [(last, r * n_vec + n_vec - 1)])
    holders, step = [n_vec - 1], n_vec // 2
    while step > 1:
        part += lax.ppermute(part, VEC, [(i, i ^ step) for i in holders])
        holders += [i ^ step for i in holders]
        step //= 2
    half = cross_rows // 2
    def of_core(c):
        return jnp.concatenate([part[c * width : (c + 1) * width], part[2 * width + c * half : 2 * width + (c + 1) * half]])
    mine = jnp.where(core == 1, of_core(1), lax.ppermute(of_core(0), VEC, [(i, i ^ 1) for i in holders]))
    mine = jnp.stack([mine] + [swapped(mine, ROW, q) for q in range(1, n_row)])
    theirs = swapped(mine, VEC, 1)
    tails = [jnp.concatenate(list(t[:, :width]), axis=1) for t in (mine, theirs)]
    pieces = jnp.where(core == 1, jnp.stack([theirs, mine], 1), jnp.stack([mine, theirs], 1))[:, :, width:]
    pieces = jnp.concatenate([lax.dynamic_index_in_dim(pieces, row ^ q, 0) for q in range(n_row)])
    cross = pieces.reshape(2, width, width)

    evens = [ritz] + [swapped(ritz, VEC, k) for k in range(2, n_vec, 2)]
    cut = len(evens) // 2
    def gather(own):
        own = jnp.concatenate(own, axis=1)
        even = jnp.concatenate([own] + [swapped(own, ROW, q) for q in range(1, n_row)], axis=0)
        return even, swapped(even, VEC, 1)

    turned = jnp.concatenate(
        [lax.dynamic_slice_in_dim(filtered, (row ^ q) * block, block, 1) for q in range(n_row)], axis=1
    )
    cols = split_array(panel_cols)
    flags = jnp.stack([is_last.astype(jnp.int32), core])
    far, near = gather(evens[cut:]), gather(evens[:cut])
    far, _ = columns(flags, turned, cols, tails, cross, panel_inverse, *far)
    near, power = columns(flags, turned, cols, tails, cross, panel_inverse, *near)

    power = power[:1, :own_cols]
    out = jnp.zeros((n_vec * rows, own_cols), jnp.float32)
    put = lambda out, value, k: lax.dynamic_update_slice_in_dim(out, value * power, (vec ^ k) * rows, 0)
    offsets = [2 * j + odd for odd in range(2) for j in range(cut)]
    for values, base in ((far, 2 * cut), (near, 0)):
        for i, k in enumerate(offsets):
            value = values[:, i * own_cols : (i + 1) * own_cols]
            if base + k:
                value = swapped(value.astype(jnp.float16), VEC, base + k).astype(jnp.float32)
            out = put(out, value, base + k)
    return out


def solution(mesh):
    in_specs = (P((ROW, VEC), None), P(ROW, VEC), P((ROW, VEC), None), P())
    return jax.shard_map(on_device, mesh=mesh, in_specs=in_specs, out_specs=P(ROW, VEC), check_vma=False)
```

```python
import functools

import jax
import jax.numpy as jnp
from jax import lax
from jax.experimental import pallas as pl
from jax.experimental.pallas import tpu as pltpu
from jax.sharding import PartitionSpec as P

ROW, VEC = "row", "vec"
TILE = 256
VMEM_LIMIT = 48 * 1024 * 1024


def swapped(value, axis, offset):
    return lax.ppermute(value, axis, [(i, i ^ offset) for i in range(lax.axis_size(axis))])


def split(value):
    high = value.astype(jnp.bfloat16)
    return high, (value - high.astype(jnp.float32)).astype(jnp.bfloat16)


def split_array(value):
    high = lax.reduce_precision(value, 8, 7)
    return high.astype(jnp.bfloat16), (value - high).astype(jnp.bfloat16)


def mul(a, b):
    return jnp.dot(a, b, preferred_element_type=jnp.float32)


def mul3(a, b):
    return mul(a[0], b[0]) + (mul(a[0], b[1]) + mul(a[1], b[0]))


def rotate_kernel(n_row, flags, filtered, *refs):
    even, odd, out, peak = refs[:n_row], refs[n_row : 2 * n_row], refs[-2], refs[-1]
    block, half = even[0].shape
    for piece, ritz in enumerate((even, odd)):
        where = pl.ds(piece * half, half)

        @pl.loop(0, out.shape[0] // TILE)
        def _(i):
            rows = pl.ds(pl.multiple_of(i * TILE, TILE), TILE)
            total = None
            for q in range(n_row):
                start = pl.multiple_of((flags[2] ^ q) * block, block)
                term = mul(filtered[rows, pl.ds(start, block)], ritz[q][...])
                total = term if total is None else total + term
            out[rows, where] = total

        most = functools.reduce(
            jnp.maximum, [jnp.max(jnp.abs(r[...].astype(jnp.float32)), axis=0, keepdims=True) for r in ritz]
        )
        peak[:, where] = jnp.broadcast_to(most, (peak.shape[0], half))


def finish_kernel(n_row, width, depth, first, flags, rotated, peak, cols_high, cols_low, inverse, *refs):
    refs = list(refs)
    take = lambda: [refs.pop(0) for _ in range(n_row)]
    outer, inner, even, odd = take(), take(), take(), take()
    out, power, solved, cross, high_ref, low_ref = refs
    half = out.shape[1] // 2
    whole = even[0].shape[1]
    block = even[0].shape[0]
    cross_rows = cross.shape[0] // n_row

    def tail(parts):
        for piece, ritz in enumerate((even, odd)):
            total = None
            for q in range(n_row):
                term = mul(parts[q][: 2 * width, :], ritz[q][:, first : first + half])
                total = term if total is None else total + term
            solved[:, piece * half : (piece + 1) * half] = total
        for q in range(n_row):
            start = pl.multiple_of((flags[2] ^ q) * cross_rows, cross_rows)
            cross[pl.ds(start, cross_rows), :] = parts[q][2 * width :, :]

    pl.when(flags[1] == 1)(lambda: tail(outer))
    pl.when(flags[1] == 0)(lambda: tail(inner))

    if block == 2 * width:
        between = cross[:, :width], cross[:, width:]
    else:
        between = cross[:width, :], cross[width:, :]
    last = mul3(split(inverse[1]), split(solved[width:, :]))
    middle = solved[:width, :] - mul3(between, split(last))
    solved[width:, :] = last
    solved[:width, :] = mul3(split(inverse[0]), split(middle))
    high_ref[...], low_ref[...] = split(solved[...])
    most = jnp.concatenate([peak[0:1, first : first + half], peak[0:1, whole + first : whole + first + half]], axis=1)
    bound = 8.0 * depth * most + 2.0 * width * jnp.max(jnp.abs(solved[...]), axis=0, keepdims=True)
    exponent = 14.0 - jnp.floor(jnp.log2(jnp.maximum(bound, 1e-30)))
    scale = jnp.exp2(exponent)
    power[...] = jnp.broadcast_to(jnp.exp2(-exponent), power.shape)

    rows = out.shape[0]
    for piece in range(2):
        where = slice(piece * half, (piece + 1) * half)
        start = piece * whole + first

        @pl.loop(0, rows // TILE)
        def _(i):
            at = pl.ds(pl.multiple_of(i * TILE, TILE), TILE)
            total = mul(cols_high[at, :], high_ref[:, where])
            total += mul(cols_high[at, :], low_ref[:, where]) + mul(cols_low[at, :], high_ref[:, where])
            out[at, where] = (rotated[at, start : start + half] - total) * scale[:, where]

    @pl.when(flags[0] == 1)
    def _():
        out[rows - 2 * width :, :] = solved[...] * scale


def call(kernel, flags, inputs, out_shape, scratch, flops):
    return pl.pallas_call(
        kernel,
        in_specs=[pl.BlockSpec(memory_space=pltpu.SMEM)] + [pl.BlockSpec(memory_space=pltpu.VMEM)] * len(inputs),
        out_specs=[pl.BlockSpec(memory_space=pltpu.VMEM)] * len(out_shape),
        out_shape=out_shape,
        scratch_shapes=scratch,
        compiler_params=pltpu.CompilerParams(vmem_limit_bytes=VMEM_LIMIT),
        cost_estimate=pl.CostEstimate(
            flops=flops, bytes_accessed=sum(a.nbytes for a in inputs), transcendentals=0
        ),
    )(flags, *inputs)


def on_device(filtered, ritz, panel_cols, panel_inverse):
    rows, depth = filtered.shape
    width = panel_inverse.shape[1]
    n_row, n_vec = lax.axis_size(ROW), lax.axis_size(VEC)
    row, vec = lax.axis_index(ROW), lax.axis_index(VEC)
    core = vec % 2
    block, own_cols = ritz.shape
    is_last = (row == n_row - 1) & (vec == n_vec - 1)
    last = n_row * n_vec - 1
    lower = rows - 2 * width

    evens = [ritz] + [swapped(ritz, VEC, k) for k in range(2, n_vec, 2)]
    cut = len(evens) // 2

    cross = jnp.concatenate(split_array(panel_cols[lower : lower + width, width:]), axis=1 if block == 2 * width else 0)
    cross_rows = cross.shape[0] // n_row
    def part_of(r):
        return jnp.concatenate(
            [filtered[lower:, r * block : (r + 1) * block], cross[r * cross_rows : (r + 1) * cross_rows]], axis=0
        )
    part = jnp.where(is_last, part_of(n_row - 1), jnp.zeros((), filtered.dtype))
    for r in range(n_row - 1):
        part += lax.ppermute(part_of(r), (ROW, VEC), [(last, r * n_vec + n_vec - 1)])
    holders, step = [n_vec - 1], n_vec // 2
    while step > 1:
        part += lax.ppermute(part, VEC, [(i, i ^ step) for i in holders])
        holders += [i ^ step for i in holders]
        step //= 2
    outer = [part] + [
        lax.ppermute(part, (ROW, VEC), [(r * n_vec + i, (r ^ q) * n_vec + i) for r in range(n_row) for i in holders])
        for q in range(1, n_row)
    ]
    inner = [lax.ppermute(p, VEC, [(i, i ^ 1) for i in holders]) for p in outer]

    own = jnp.concatenate(evens, axis=1)
    even = [own] + [swapped(own, ROW, q) for q in range(1, n_row)]
    odd = [swapped(e, VEC, 1) for e in even]

    flags = jnp.stack([is_last.astype(jnp.int32), core, row])
    count = n_vec * own_cols
    rotated, peak = call(
        functools.partial(rotate_kernel, n_row), flags, [filtered, *even, *odd],
        [jax.ShapeDtypeStruct((rows, count), jnp.float32), jax.ShapeDtypeStruct((8, count), jnp.float32)],
        [], 2 * rows * depth * count,
    )
    cols = split_array(panel_cols)

    def finish(flags, first):
        return call(
            functools.partial(finish_kernel, n_row, width, depth, first), flags,
            [rotated, peak, *cols, panel_inverse, *outer, *inner, *even, *odd],
            [jax.ShapeDtypeStruct((rows, count // 2), jnp.float32), jax.ShapeDtypeStruct((8, count // 2), jnp.float32)],
            [pltpu.VMEM((2 * width, count // 2), jnp.float32), pltpu.VMEM(cross.shape, jnp.bfloat16)]
            + [pltpu.VMEM((2 * width, count // 2), jnp.bfloat16)] * 2,
            width * (depth + 6 * rows) * count,
        )

    offsets = [2 * j + side for side in range(2) for j in range(cut)]
    piece = lambda values, i: values[:, i * own_cols : (i + 1) * own_cols]
    far, _ = finish(flags, cut * own_cols)
    far = [piece(far, i).astype(jnp.float16) for i in range(2 * cut)]
    far, flags = lax.optimization_barrier((far, flags))
    sent = {2 * cut + k: swapped(f, VEC, 2 * cut + k) for f, k in zip(far, offsets)}
    near, power = finish(flags, 0)
    power = power[:1, :own_cols]
    for i, k in enumerate(offsets):
        sent[k] = swapped(piece(near, i).astype(jnp.float16), VEC, k) if k else piece(near, i)
    out = jnp.zeros((n_vec * rows, own_cols), jnp.float32)
    for k, value in sorted(sent.items()):
        out = lax.dynamic_update_slice_in_dim(out, value.astype(jnp.float32) * power, (vec ^ k) * rows, 0)
    return out


def solution(mesh):
    in_specs = (P((ROW, VEC), None), P(ROW, VEC), P((ROW, VEC), None), P())
    return jax.shard_map(on_device, mesh=mesh, in_specs=in_specs, out_specs=P(ROW, VEC), check_vma=False)
```

```python
import functools

import jax
import jax.numpy as jnp
from jax import lax
from jax.experimental import pallas as pl
from jax.experimental.pallas import tpu as pltpu
from jax.sharding import PartitionSpec as P

ROW, VEC = "row", "vec"
VMEM_LIMIT = 16 * 1024 * 1024


def swapped(value, axis, offset):
    return lax.ppermute(value, axis, [(i, i ^ offset) for i in range(lax.axis_size(axis))])


def steps_of(size):
    return [1 << i for i in range(size.bit_length() - 1)]


def split(value):
    high = value.astype(jnp.bfloat16)
    return high, (value - high.astype(jnp.float32)).astype(jnp.bfloat16)


def split_array(value):
    high = lax.reduce_precision(value, 8, 7)
    return high.astype(jnp.bfloat16), (value - high).astype(jnp.bfloat16)


def mul(a, b):
    return jnp.dot(a, b, preferred_element_type=jnp.float32)


def mul3(a, b):
    left = jnp.concatenate([a[0], a[0], a[1]], axis=1)
    return mul(left, jnp.concatenate([b[0], b[1], b[0]], axis=0))


def side_kernel(*refs):
    *parts, first, second = refs
    cut, width = len(parts) // 2, parts[0].shape[1]
    for i, part in enumerate(parts):
        (first, second)[i // cut][:, i % cut * width : (i % cut + 1) * width] = part[...]


def rotate_kernel(places, flags, filtered, *refs):
    *parts, out, ritz, peak, rows, sems = refs
    n_row = len(places[0])
    block, half = ritz.shape[0] // n_row, ritz.shape[1] // 4
    copies = []
    for i, order in enumerate(places * 2):
        own = parts[i * len(parts) // 4 : (i + 1) * len(parts) // 4]
        for j, q in enumerate(order):
            part, place = own[j * len(own) // n_row], j % (n_row // len(own))
            into = ritz.at[pl.ds(q * block, block), pl.ds(i * half, half)]
            source = part.at[pl.ds(place * block, block), :]
            copies.append(pltpu.make_async_copy(source, into, sems.at[len(copies)]))
    chunk = rows.shape[0] // 4
    for i in range(4):
        at = pl.ds(i * chunk, chunk)
        copies.append(pltpu.make_async_copy(filtered.at[at, :], rows.at[at, :], sems.at[len(copies)]))
    for copy in copies:
        copy.start()
    for copy in copies[:-4]:
        copy.wait()
    for i in range(4):
        copies[4 * n_row + i].wait()
        at = slice(i * chunk, (i + 1) * chunk)
        left = jnp.concatenate(
            [rows[at, pl.ds(pl.multiple_of((flags[2] ^ q) * block, block), block)] for q in range(n_row)], axis=1
        )
        out[at, :] = mul(left, ritz[...])
    most = jnp.max(jnp.abs(ritz[...].astype(jnp.float32)), axis=0, keepdims=True)
    peak[...] = jnp.broadcast_to(most, peak.shape)


def solve_kernel(n_row, first, flags, inverse, ritz, *refs):
    tails, (out, rows, cross, solved, sems) = refs[:n_row], refs[n_row:]
    width = inverse.shape[1]
    half = out.shape[1] // 2
    block = ritz.shape[0] // n_row
    cross_rows = cross.shape[0] // n_row
    copies = []
    for q in range(n_row):
        into = rows.at[:, pl.ds(q * block, block)]
        copies.append(pltpu.make_async_copy(tails[q].at[pl.ds(0, 2 * width), :], into, sems.at[2 * q]))
        into = cross.at[pl.ds(pl.multiple_of((flags[2] ^ q) * cross_rows, cross_rows), cross_rows), :]
        copies.append(
            pltpu.make_async_copy(tails[q].at[pl.ds(2 * width, cross_rows), :], into, sems.at[2 * q + 1])
        )
    for copy in copies:
        copy.start()
    for copy in copies:
        copy.wait()
    for piece in range(2):
        start = first + 2 * piece * half
        solved[:, piece * half : (piece + 1) * half] = mul(rows[...], ritz[:, start : start + half])
    if block == 2 * width:
        between = cross[:, :width], cross[:, width:]
    else:
        between = cross[:width, :], cross[width:, :]
    last = mul3(split(inverse[1]), split(solved[width:, :]))
    middle = solved[:width, :] - mul3(between, split(last))
    after = mul3(split(inverse[0]), split(middle))
    out[width : 2 * width, :], out[3 * width :, :] = split(last)
    out[:width, :], out[2 * width : 3 * width, :] = split(after)


def correct_kernel(width, depth, first, flags, rotated, peak, cols_high, cols_low, own, other, out, power, solved):
    rows, count = out.shape
    half, size = count // 2, 2 * width

    @pl.when(flags[1] == 1)
    def _():
        solved[...] = own[...]

    @pl.when(flags[1] == 0)
    def _():
        solved[:, :half] = other[:, half:]
        solved[:, half:] = other[:, :half]

    panels = solved[:size, :].astype(jnp.float32) + solved[size:, :].astype(jnp.float32)
    most = jnp.concatenate([peak[0:1, i : i + half] for i in (first, first + 2 * half)], axis=1)
    bound = 8.0 * depth * most + size * jnp.max(jnp.abs(panels), axis=0, keepdims=True)
    exponent = 14.0 - jnp.floor(jnp.log2(jnp.maximum(bound, 1e-30)))
    scale = jnp.exp2(exponent)
    power[...] = jnp.broadcast_to(jnp.exp2(-exponent), power.shape)
    left = jnp.concatenate([cols_high[...], cols_high[...], cols_low[...]], axis=1)
    for piece in range(2):
        start = first + 2 * piece * half
        where = slice(piece * half, (piece + 1) * half)
        right = jnp.concatenate([solved[:, where], solved[:size, where]], axis=0)
        out[:, where] = (rotated[:, start : start + half] - mul(left, right)) * scale[:, where]

    @pl.when(flags[0] == 1)
    def _():
        out[rows - size :, :] = panels * scale


def place_kernel(ks, flags, power, *refs):
    out, ready, sems = refs[-3:]
    copies = []
    for i, k in enumerate(ks):
        size, width = refs[i].shape
        ready[i] = refs[i][...] * power[0:1, :width]
        into = out.at[pl.ds(pl.multiple_of((flags[3] ^ k) * size, size), size), :]
        copies.append(pltpu.make_async_copy(ready.at[i], into, sems.at[i]))
        copies[i].start()
    for copy in copies:
        copy.wait()


def call(kernel, flags, inputs, out_shape, scratch):
    spec = lambda space: pl.BlockSpec(memory_space=space)
    specs, arrays, scalars = [], [], [] if flags is None else [flags]
    for value in inputs:
        group = value if isinstance(value, list) else [value]
        specs += [spec(pltpu.HBM if isinstance(value, list) else pltpu.VMEM)] * len(group)
        arrays += group
    return pl.pallas_call(
        kernel,
        in_specs=[spec(pltpu.SMEM)] * len(scalars) + specs,
        out_specs=[spec(pltpu.VMEM)] * len(out_shape),
        out_shape=[jax.ShapeDtypeStruct(*s) for s in out_shape],
        scratch_shapes=scratch,
        compiler_params=pltpu.CompilerParams(vmem_limit_bytes=VMEM_LIMIT),
        cost_estimate=pl.CostEstimate(flops=1, bytes_accessed=1, transcendentals=0),
    )(*scalars, *arrays)


def on_device(filtered, ritz, panel_cols, panel_inverse):
    rows, depth = filtered.shape
    width = panel_inverse.shape[1]
    n_row, n_vec = lax.axis_size(ROW), lax.axis_size(VEC)
    row, vec = lax.axis_index(ROW), lax.axis_index(VEC)
    block, own_cols = ritz.shape
    is_last = (row == n_row - 1) & (vec == n_vec - 1)
    last = n_row * n_vec - 1
    lower = rows - 2 * width
    cut = n_vec // 4
    f32, bf16 = jnp.float32, jnp.bfloat16
    holders = range(1, n_vec, 2)

    flags = jnp.stack([is_last.astype(jnp.int32), vec & 1, row, vec])
    filtered, ritz, panel_cols, flags, is_last = lax.optimization_barrier((filtered, ritz, panel_cols, flags, is_last))
    cols = split_array(panel_cols)

    cross = jnp.concatenate(split_array(panel_cols[lower : lower + width, width:]), axis=1 if block == 2 * width else 0)
    cross_rows = cross.shape[0] // n_row
    def part_of(r):
        return jnp.concatenate(
            [filtered[lower:, r * block : (r + 1) * block], cross[r * cross_rows : (r + 1) * cross_rows]], axis=0
        )
    evens = [ritz] + [swapped(ritz, VEC, k) for k in range(2, n_vec, 2)]
    parts = [lax.ppermute(part_of(r), (ROW, VEC), [(last, r * n_vec + n_vec - 1)]) for r in range(n_row - 1)]
    evens, parts = lax.optimization_barrier((evens, parts))

    part = sum(parts, jnp.where(is_last, part_of(n_row - 1), jnp.zeros((), bf16)))
    halves = call(side_kernel, None, evens[cut:] + evens[:cut], [((block, cut * own_cols), bf16)] * 2, [])
    halves, places = [[h] for h in halves], [[0], [0]]
    steps, downs, sources = steps_of(n_row), steps_of(n_vec)[:0:-1], [n_vec - 1]
    for i in range(max(len(steps), len(downs))):
        if i < len(steps):
            for which, step in enumerate((steps[i], steps[-1 - i])):
                known = jnp.concatenate(halves[which], axis=0)
                halves[which] = [known, swapped(known, ROW, step)]
                places[which] = places[which] + [q ^ step for q in places[which]]
        if i < len(downs):
            part += lax.ppermute(part, VEC, [(v, v ^ downs[i]) for v in sources])
            sources += [v ^ downs[i] for v in sources]
        if i == 0:
            halves, part, cols = lax.optimization_barrier((halves, part, cols))
    odds = [[swapped(h, VEC, 1) for h in half] for half in halves]

    tails = [part] + [
        lax.ppermute(part, (ROW, VEC), [(r * n_vec + i, (r ^ q) * n_vec + i) for r in range(n_row) for i in holders])
        for q in range(1, n_row)
    ]
    count = n_vec * own_cols // 2

    rotated, gathered, peak = call(
        functools.partial(rotate_kernel, places), flags, [[filtered, *sum(halves + odds, [])]],
        [((rows, 2 * count), f32), ((depth, 2 * count), bf16), ((8, 2 * count), f32)],
        [pltpu.VMEM((rows, depth), bf16), pltpu.SemaphoreType.DMA((4 + 4 * n_row,))],
    )

    def solve(first):
        own, = call(
            functools.partial(solve_kernel, n_row, first), flags, [panel_inverse, gathered, tails],
            [((4 * width, count), bf16)],
            [
                pltpu.VMEM((2 * width, depth), bf16), pltpu.VMEM(cross.shape, bf16),
                pltpu.VMEM((2 * width, count), f32), pltpu.SemaphoreType.DMA((2 * n_row,)),
            ],
        )
        return own, lax.ppermute(own, VEC, [(i, i ^ 1) for i in holders])

    def correct(first, solved):
        return call(
            functools.partial(correct_kernel, width, depth, first), flags,
            [rotated, peak, *cols, *solved],
            [((rows, count), f32), ((8, count), f32)], [pltpu.VMEM((4 * width, count), bf16)],
        )

    tails, rotated, gathered, peak = lax.optimization_barrier((tails, rotated, gathered, peak))

    piece = lambda values, i: values[:, i * own_cols : (i + 1) * own_cols].astype(jnp.float16)
    solved = [solve(0), solve(count // 2)]
    values, _ = correct(0, solved[0])
    values = [piece(values, i) for i in range(2 * cut)]
    values, solved = lax.optimization_barrier((values, solved))
    sent = {}
    for i, k in enumerate(2 * cut + 2 * j + odd for odd in range(2) for j in range(cut)):
        sent[k] = swapped(values[i], VEC, k)
    values, power = correct(count // 2, solved[1])
    sent[0] = values[:, :own_cols]
    for i, k in enumerate(2 * j + odd for odd in range(2) for j in range(cut)):
        if k:
            sent[k] = swapped(piece(values, i), VEC, k)

    def place(out, ks):
        shape = jax.ShapeDtypeStruct((n_vec * rows, own_cols), f32)
        spec = lambda space: pl.BlockSpec(memory_space=space)
        return pl.pallas_call(
            functools.partial(place_kernel, ks),
            in_specs=[spec(pltpu.SMEM)] + [spec(pltpu.VMEM)] * (1 + len(ks)) + [spec(pl.ANY)] * len(out),
            out_specs=spec(pl.ANY), out_shape=shape,
            scratch_shapes=[pltpu.VMEM((len(ks), rows, own_cols), f32), pltpu.SemaphoreType.DMA((len(ks),))],
            input_output_aliases={2 + len(ks): 0} if out else {},
            compiler_params=pltpu.CompilerParams(vmem_limit_bytes=VMEM_LIMIT),
        )(flags, power, *(sent[k].astype(f32) for k in ks), *out)

    late = [k for k in sent if k >= 2 * cut or k == 2]
    return place([place([], [k for k in sent if k not in late])], late)


def solution(mesh):
    in_specs = (P((ROW, VEC), None), P(ROW, VEC), P((ROW, VEC), None), P())
    return jax.shard_map(on_device, mesh=mesh, in_specs=in_specs, out_specs=P(ROW, VEC), check_vma=False)
```

```python
import functools

import jax
import jax.numpy as jnp
from jax import lax
from jax.experimental import pallas as pl
from jax.experimental.pallas import tpu as pltpu
from jax.sharding import PartitionSpec as P

ROW, VEC = "row", "vec"
VMEM_LIMIT = 16 * 1024 * 1024


def swapped(value, axis, offset):
    return lax.ppermute(value, axis, [(i, i ^ offset) for i in range(lax.axis_size(axis))])


def steps_of(size):
    return [1 << i for i in range(size.bit_length() - 1)]


def split(value):
    high = value.astype(jnp.bfloat16)
    return high, (value - high.astype(jnp.float32)).astype(jnp.bfloat16)


def split_array(value):
    high = lax.reduce_precision(value, 8, 7)
    return high.astype(jnp.bfloat16), (value - high).astype(jnp.bfloat16)


def mul(a, b):
    return jnp.dot(a, b, preferred_element_type=jnp.float32)


def mul3(a, b):
    left = jnp.concatenate([a[0], a[0], a[1]], axis=1)
    return mul(left, jnp.concatenate([b[0], b[1], b[0]], axis=0))


def side_kernel(*refs):
    *parts, first, second = refs
    cut, width = len(parts) // 2, parts[0].shape[1]
    for i, part in enumerate(parts):
        (first, second)[i // cut][:, i % cut * width : (i % cut + 1) * width] = part[...]


def gathered(parts, places, block):
    each = parts[0].shape[0] // block
    where = {q: (parts[j // each], j % each) for j, q in enumerate(places)}
    return jnp.concatenate([p[i * block : (i + 1) * block, :] for p, i in (where[q] for q in sorted(where))], axis=0)


def rotate_kernel(places, flags, own, other, *refs):
    *parts, out, peak = refs
    n_row, each, rows = len(places[0]), len(parts) // 2, own.shape[0]
    block = own.shape[1] // n_row
    for i, order in enumerate(places):
        ritz = gathered(parts[i * each : (i + 1) * each], order, block)
        where = slice(i * ritz.shape[1], (i + 1) * ritz.shape[1])
        for filtered, core in ((own, flags[1]), (other, 1 - flags[1])):
            left = jnp.concatenate(
                [filtered[:, pl.ds(pl.multiple_of((flags[2] ^ q) * block, block), block)] for q in range(n_row)], axis=1
            )
            out[pl.ds(pl.multiple_of(core * rows, rows), rows), where] = mul(left, ritz)
        most = jnp.max(jnp.abs(ritz.astype(jnp.float32)), axis=0, keepdims=True)
        peak[:, where] = jnp.broadcast_to(most, (peak.shape[0], most.shape[1]))


def solve_kernel(places, flags, inverse, *refs):
    n_row = len(places[0])
    outer, inner, parts, (out, cross, solved) = refs[:n_row], refs[n_row : 2 * n_row], refs[2 * n_row : -3], refs[-3:]
    width = inverse.shape[1]
    block = outer[0].shape[1]
    cross_rows = cross.shape[0] // n_row
    each = len(parts) // 2

    def tail(sent):
        rows = jnp.concatenate([t[: 2 * width, :] for t in sent], axis=1)
        for q in range(n_row):
            start = pl.multiple_of((flags[2] ^ q) * cross_rows, cross_rows)
            cross[pl.ds(start, cross_rows), :] = sent[q][2 * width :, :]
        for i, order in enumerate(places):
            ritz = gathered(parts[i * each : (i + 1) * each], order, block)
            solved[:, i * ritz.shape[1] : (i + 1) * ritz.shape[1]] = mul(rows, ritz)

    pl.when(flags[1] == 1)(lambda: tail(outer))
    pl.when(flags[1] == 0)(lambda: tail(inner))
    if block == 2 * width:
        between = cross[:, :width], cross[:, width:]
    else:
        between = cross[:width, :], cross[width:, :]
    last = mul3(split(inverse[1]), split(solved[width:, :]))
    middle = solved[:width, :] - mul3(between, split(last))
    after = mul3(split(inverse[0]), split(middle))
    out[width : 2 * width, :], out[3 * width :, :] = split(last)
    out[:width, :], out[2 * width : 3 * width, :] = split(after)


def correct_kernel(depth, which, flags, rotated, peak, own, other, solved, out, power):
    rows, size = own.shape[0], own.shape[1] // 2
    half = out.shape[1]
    where = slice(which * half, (which + 1) * half)
    panels = solved[:size, where].astype(jnp.float32) + solved[size:, where].astype(jnp.float32)
    bound = 8.0 * depth * peak[0:1, where] + size * jnp.max(jnp.abs(panels), axis=0, keepdims=True)
    exponent = 14.0 - jnp.floor(jnp.log2(jnp.maximum(bound, 1e-30)))
    scale = jnp.exp2(exponent)
    power[...] = jnp.broadcast_to(jnp.exp2(-exponent), power.shape)
    right = jnp.concatenate([solved[:, where], solved[:size, where]], axis=0)
    for cols, core in ((own, flags[1]), (other, 1 - flags[1])):
        at = pl.ds(pl.multiple_of(core * rows, rows), rows)
        left = jnp.concatenate([cols[:, :size], cols[...]], axis=1)
        out[at, :] = (rotated[at, where] - mul(left, right)) * scale

    @pl.when(flags[0] == 1)
    def _():
        out[2 * rows - size :, :] = panels * scale


def place_kernel(ks, flags, power, *refs):
    out, ready, sems = refs[-3:]
    size, width = ready.shape[1:]
    parts = list(refs)
    copies = []
    for i, (k, count) in enumerate(ks):
        for j in range(count):
            part = parts.pop(0)
            step = part.shape[0]
            ready[i, j * step : (j + 1) * step, :] = part[...] * power[0:1, :width]
        into = out.at[pl.ds(pl.multiple_of(((flags[3] ^ k) >> 1) * size, size), size), :]
        copies.append(pltpu.make_async_copy(ready.at[i], into, sems.at[i]))
        copies[i].start()
    for copy in copies:
        copy.wait()


def call(kernel, flags, inputs, out_shape, scratch):
    spec = lambda space: pl.BlockSpec(memory_space=space)
    specs, arrays, scalars = [], [], [] if flags is None else [flags]
    for value in inputs:
        group = value if isinstance(value, list) else [value]
        specs += [spec(pltpu.HBM if isinstance(value, list) else pltpu.VMEM)] * len(group)
        arrays += group
    return pl.pallas_call(
        kernel,
        in_specs=[spec(pltpu.SMEM)] * len(scalars) + specs,
        out_specs=[spec(pltpu.VMEM)] * len(out_shape),
        out_shape=[jax.ShapeDtypeStruct(*s) for s in out_shape],
        scratch_shapes=scratch,
        compiler_params=pltpu.CompilerParams(vmem_limit_bytes=VMEM_LIMIT),
        cost_estimate=pl.CostEstimate(flops=1, bytes_accessed=1, transcendentals=0),
    )(*scalars, *arrays)


def on_device(filtered, ritz, panel_cols, panel_inverse):
    rows, depth = filtered.shape
    width = panel_inverse.shape[1]
    n_row, n_vec = lax.axis_size(ROW), lax.axis_size(VEC)
    row, vec = lax.axis_index(ROW), lax.axis_index(VEC)
    block, own_cols = ritz.shape
    is_last = (row == n_row - 1) & (vec == n_vec - 1)
    last = n_row * n_vec - 1
    lower = rows - 2 * width
    cut = n_vec // 4
    f32, bf16 = jnp.float32, jnp.bfloat16
    holders = range(1, n_vec, 2)

    last_chip = (row == n_row - 1) & (vec >= n_vec - 2)
    flags = jnp.stack([last_chip.astype(jnp.int32), vec & 1, row, vec])
    filtered, ritz, panel_cols, flags, is_last = lax.optimization_barrier((filtered, ritz, panel_cols, flags, is_last))

    cross = jnp.concatenate(split_array(panel_cols[lower : lower + width, width:]), axis=1 if block == 2 * width else 0)
    cross_rows = cross.shape[0] // n_row
    def part_of(r):
        return jnp.concatenate(
            [filtered[lower:, r * block : (r + 1) * block], cross[r * cross_rows : (r + 1) * cross_rows]], axis=0
        )
    evens = {0: ritz}
    for step in steps_of(n_vec)[:0:-1]:
        evens.update({k | step: swapped(value, VEC, step) for k, value in evens.items()})
    evens = [evens[k] for k in sorted(evens)]
    parts = [lax.ppermute(part_of(r), (ROW, VEC), [(last, r * n_vec + n_vec - 1)]) for r in range(n_row - 1)]
    evens, parts, shared, cols = lax.optimization_barrier((evens, parts, filtered, panel_cols))
    shared = swapped(shared, VEC, 1)
    cols = jnp.concatenate(split_array(cols), axis=1)
    cols = [cols, swapped(cols, VEC, 1)]

    part = sum(parts, jnp.where(is_last, part_of(n_row - 1), jnp.zeros((), bf16)))
    halves = call(side_kernel, None, evens[cut:] + evens[:cut], [((block, cut * own_cols), bf16)] * 2, [])
    halves, places = [[h] for h in halves], [[0], [0]]
    steps, downs, sources = steps_of(n_row), steps_of(n_vec)[:0:-1], [n_vec - 1]
    for i in range(max(len(steps), len(downs))):
        if i < len(steps):
            for which, step in enumerate((steps[i], steps[-1 - i])):
                known = jnp.concatenate(halves[which], axis=0)
                halves[which] = [known, swapped(known, ROW, step)]
                places[which] = places[which] + [q ^ step for q in places[which]]
        if i < len(downs):
            part += lax.ppermute(part, VEC, [(v, v ^ downs[i]) for v in sources])
            sources += [v ^ downs[i] for v in sources]
        if i == 0:
            halves = lax.optimization_barrier(halves)
    across = lambda p: lax.ppermute(p, VEC, [(i, i ^ 1) for i in holders])
    outer = [part] + [
        lax.ppermute(part, (ROW, VEC), [(r * n_vec + i, (r ^ q) * n_vec + i) for r in range(n_row) for i in holders])
        for q in range(1, n_row)
    ]
    inner = [across(part)]
    count = n_vec * own_cols // 2
    parts = sum(halves, [])
    rotated, peak = call(
        functools.partial(rotate_kernel, places), flags, [filtered, shared, *parts],
        [((2 * rows, count), f32), ((8, count), f32)], [],
    )
    outer, rotated, peak, cols = lax.optimization_barrier((outer, rotated, peak, cols))
    inner += [across(p) for p in outer[1:]]

    solved, = call(
        functools.partial(solve_kernel, places), flags, [panel_inverse, *outer, *inner, *parts],
        [((4 * width, count), bf16)], [pltpu.VMEM(cross.shape, bf16), pltpu.VMEM((2 * width, count), f32)],
    )

    def correct(which, solved):
        return call(
            functools.partial(correct_kernel, depth, which), flags, [rotated, peak, *cols, solved],
            [((2 * rows, count // 2), f32), ((8, count // 2), f32)], [],
        )

    piece = lambda values, i: values[:, i * own_cols : (i + 1) * own_cols]
    values, _ = correct(0, solved)
    values = [piece(values, j).astype(jnp.float16) for j in range(cut)]
    values, solved = lax.optimization_barrier((values, solved))
    far = {2 * (cut + j): [swapped(values[j], VEC, 2 * (cut + j))] for j in range(cut)}
    values, power = correct(1, solved)
    near = {}
    for j in range(1, cut):
        value = piece(values, j).astype(jnp.float16)
        near[2 * j] = [swapped(v, VEC, 2 * j) for v in (value[:rows], value[rows:])]
    near[0] = [piece(values, 0)]

    shape = jax.ShapeDtypeStruct((n_vec * rows, own_cols), f32)
    spec = lambda space: pl.BlockSpec(memory_space=space)

    def place(blocks, out):
        parts = sum(blocks.values(), [])
        return pl.pallas_call(
            functools.partial(place_kernel, [(k, len(v)) for k, v in blocks.items()]),
            in_specs=[spec(pltpu.SMEM)] + [spec(pltpu.VMEM)] * (1 + len(parts)) + [spec(pl.ANY)] * len(out),
            out_specs=spec(pl.ANY), out_shape=shape,
            scratch_shapes=[
                pltpu.VMEM((len(blocks), 2 * rows, own_cols), f32), pltpu.SemaphoreType.DMA((len(blocks),))
            ],
            input_output_aliases={2 + len(parts): 0} if out else {},
            compiler_params=pltpu.CompilerParams(vmem_limit_bytes=VMEM_LIMIT),
            cost_estimate=pl.CostEstimate(flops=1, bytes_accessed=1, transcendentals=0),
        )(flags, power, *(v.astype(f32) for v in parts), *out)

    return place(far, [place(near, [])])


def solution(mesh):
    in_specs = (P((ROW, VEC), None), P(ROW, VEC), P((ROW, VEC), None), P())
    return jax.shard_map(on_device, mesh=mesh, in_specs=in_specs, out_specs=P(ROW, VEC), check_vma=False)
```

```python
import functools

import jax
import jax.numpy as jnp
from jax import lax
from jax.experimental import pallas as pl
from jax.experimental.pallas import tpu as pltpu
from jax.sharding import PartitionSpec as P

ROW, VEC = "row", "vec"
VMEM_LIMIT = 16 * 1024 * 1024


def swapped(value, axis, offset):
    return lax.ppermute(value, axis, [(i, i ^ offset) for i in range(lax.axis_size(axis))])


def steps_of(size):
    return [1 << i for i in range(size.bit_length() - 1)]


def split(value):
    high = value.astype(jnp.bfloat16)
    return high, (value - high.astype(jnp.float32)).astype(jnp.bfloat16)


def split_array(value):
    high = lax.reduce_precision(value, 8, 7)
    return high.astype(jnp.bfloat16), (value - high).astype(jnp.bfloat16)


def mul(a, b):
    return jnp.dot(a, b, preferred_element_type=jnp.float32)


def mul3(a, b):
    left = jnp.concatenate([a[0], a[0], a[1]], axis=1)
    return mul(left, jnp.concatenate([b[0], b[1], b[0]], axis=0))


def side_kernel(order, parts, first, second):
    cut, width = len(order) // 2, parts.shape[2]
    for i, j in enumerate(order):
        (first, second)[i // cut][:, i % cut * width : (i % cut + 1) * width] = parts[j]


def gathered(parts, places, block):
    each = parts[0].shape[0] // block
    where = {q: (parts[j // each], j % each) for j, q in enumerate(places)}
    return jnp.concatenate([p[i * block : (i + 1) * block, :] for p, i in (where[q] for q in sorted(where))], axis=0)


def rotate_kernel(places, flags, own, other, *refs):
    *parts, out, peak = refs
    n_row, each, rows = len(places[0]), len(parts) // 2, own.shape[0]
    block = own.shape[1] // n_row
    for i, order in enumerate(places):
        ritz = gathered(parts[i * each : (i + 1) * each], order, block)
        where = slice(i * ritz.shape[1], (i + 1) * ritz.shape[1])
        for filtered, core in ((own, flags[1]), (other, 1 - flags[1])):
            left = jnp.concatenate(
                [filtered[:, pl.ds(pl.multiple_of((flags[2] ^ q) * block, block), block)] for q in range(n_row)], axis=1
            )
            out[pl.ds(pl.multiple_of(core * rows, rows), rows), where] = mul(left, ritz)
        most = jnp.max(jnp.abs(ritz.astype(jnp.float32)), axis=0, keepdims=True)
        peak[:, where] = jnp.broadcast_to(most, (peak.shape[0], most.shape[1]))


def solve_kernel(places, flags, inverse, *refs):
    n_row = len(places)
    outer, inner, parts, (out, cross, solved) = refs[:n_row], refs[n_row], refs[n_row + 1 : -3], refs[-3:]
    size = outer[0].shape[0]
    width = inverse.shape[1]
    block = outer[0].shape[1]
    cross_rows = cross.shape[0] // n_row

    def tail(sent):
        rows = jnp.concatenate([t[start : start + 2 * width, :] for t, start in sent], axis=1)
        for q in range(n_row):
            start = pl.multiple_of((flags[2] ^ q) * cross_rows, cross_rows)
            t, first = sent[q]
            cross[pl.ds(start, cross_rows), :] = t[first + 2 * width : first + size, :]
        solved[...] = mul(rows, gathered(parts, places, block))

    pl.when(flags[1] == 1)(lambda: tail([(t, 0) for t in outer]))
    pl.when(flags[1] == 0)(lambda: tail([(inner, q * size) for q in range(n_row)]))
    if block == 2 * width:
        between = cross[:, :width], cross[:, width:]
    else:
        between = cross[:width, :], cross[width:, :]
    last = mul3(split(inverse[1]), split(solved[width:, :]))
    middle = solved[:width, :] - mul3(between, split(last))
    after = mul3(split(inverse[0]), split(middle))
    out[width : 2 * width, :], out[3 * width :, :] = split(last)
    out[:width, :], out[2 * width : 3 * width, :] = split(after)


def correct_kernel(depth, which, flags, rotated, peak, own, other, solved, out, power):
    rows, size = own.shape[0], own.shape[1] // 2
    half = out.shape[1]
    where = slice(which * half, (which + 1) * half)
    panels = solved[:size, :].astype(jnp.float32) + solved[size:, :].astype(jnp.float32)
    bound = 8.0 * depth * peak[0:1, where] + size * jnp.max(jnp.abs(panels), axis=0, keepdims=True)
    exponent = 14.0 - jnp.floor(jnp.log2(jnp.maximum(bound, 1e-30)))
    scale = jnp.exp2(exponent)
    power[...] = jnp.broadcast_to(jnp.exp2(-exponent), power.shape)
    right = jnp.concatenate([solved[...], solved[:size, :]], axis=0)
    for cols, core in ((own, flags[1]), (other, 1 - flags[1])):
        at = pl.ds(pl.multiple_of(core * rows, rows), rows)
        left = jnp.concatenate([cols[:, :size], cols[...]], axis=1)
        out[at, :] = (rotated[at, where] - mul(left, right)) * scale

    @pl.when(flags[0] == 1)
    def _():
        out[2 * rows - size :, :] = panels * scale


def place_kernel(ks, flags, power, *refs):
    out, ready, sems = refs[-3:]
    size, width = ready.shape[1:]
    parts = list(refs)
    copies = []
    for i, (k, count) in enumerate(ks):
        for j in range(count):
            part = parts.pop(0)
            step = part.shape[0]
            ready[i, j * step : (j + 1) * step, :] = part[...] * power[0:1, :width]
        into = out.at[pl.ds(pl.multiple_of(((flags[3] ^ k) >> 1) * size, size), size), :]
        copies.append(pltpu.make_async_copy(ready.at[i], into, sems.at[i]))
        copies[i].start()
    for copy in copies:
        copy.wait()


def call(kernel, flags, inputs, out_shape, scratch, work=1):
    spec = lambda space: pl.BlockSpec(memory_space=space)
    specs, arrays, scalars = [], [], [] if flags is None else [flags]
    for value in inputs:
        group = value if isinstance(value, list) else [value]
        specs += [spec(pltpu.HBM if isinstance(value, list) else pltpu.VMEM)] * len(group)
        arrays += group
    return pl.pallas_call(
        kernel,
        in_specs=[spec(pltpu.SMEM)] * len(scalars) + specs,
        out_specs=[spec(pltpu.VMEM)] * len(out_shape),
        out_shape=[jax.ShapeDtypeStruct(*s) for s in out_shape],
        scratch_shapes=scratch,
        compiler_params=pltpu.CompilerParams(vmem_limit_bytes=VMEM_LIMIT),
        cost_estimate=pl.CostEstimate(flops=work, bytes_accessed=1, transcendentals=0),
    )(*scalars, *arrays)


def on_device(filtered, ritz, panel_cols, panel_inverse):
    rows, depth = filtered.shape
    width = panel_inverse.shape[1]
    n_row, n_vec = lax.axis_size(ROW), lax.axis_size(VEC)
    row, vec = lax.axis_index(ROW), lax.axis_index(VEC)
    block, own_cols = ritz.shape
    is_last = (row == n_row - 1) & (vec == n_vec - 1)
    last = n_row * n_vec - 1
    lower = rows - 2 * width
    cut = n_vec // 4
    f32, bf16 = jnp.float32, jnp.bfloat16
    holders = range(1, n_vec, 2)

    last_chip = (row == n_row - 1) & (vec >= n_vec - 2)
    flags = jnp.stack([last_chip.astype(jnp.int32), vec & 1, row, vec])
    filtered, ritz, panel_cols, flags, is_last = lax.optimization_barrier((filtered, ritz, panel_cols, flags, is_last))

    cross = jnp.concatenate(split_array(panel_cols[lower : lower + width, width:]), axis=1 if block == 2 * width else 0)
    cross_rows = cross.shape[0] // n_row
    def part_of(r):
        return jnp.concatenate(
            [filtered[lower:, r * block : (r + 1) * block], cross[r * cross_rows : (r + 1) * cross_rows]], axis=0
        )
    own, evens = ritz[None], [0]
    for step in steps_of(n_vec)[:0:-1]:
        own = jnp.concatenate([own, swapped(own, VEC, step)])
        evens += [k ^ step for k in evens]
    shared = swapped(filtered, VEC, 1)
    parts = [lax.ppermute(part_of(r), (ROW, VEC), [(last, r * n_vec + n_vec - 1)]) for r in range(n_row - 1)]
    part = sum(parts, jnp.where(is_last, part_of(n_row - 1), jnp.zeros((), bf16)))
    cols = jnp.concatenate(split_array(panel_cols), axis=1)
    own, part, shared, cols = lax.optimization_barrier((own, part, shared, cols))

    order = [evens.index(2 * ((cut + i) % (2 * cut))) for i in range(2 * cut)]
    halves = call(
        functools.partial(side_kernel, order), None, [own], [((block, cut * own_cols), bf16)] * 2, []
    )
    halves, places = [[h] for h in halves], [[0], [0]]
    steps, downs, sources = steps_of(n_row), steps_of(n_vec)[:0:-1], [n_vec - 1]
    for i in range(max(len(steps), len(downs))):
        if i < len(steps):
            for which, step in enumerate((steps[i], steps[-1 - i])):
                known = jnp.concatenate(halves[which], axis=0)
                halves[which] = [known, swapped(known, ROW, step)]
                places[which] = places[which] + [q ^ step for q in places[which]]
        if i < len(downs):
            part += lax.ppermute(part, VEC, [(v, v ^ downs[i]) for v in sources])
            sources += [v ^ downs[i] for v in sources]
        if i == 0:
            halves, part, cols = lax.optimization_barrier((halves, part, cols))
            other_cols = swapped(cols, VEC, 1)
    part, other_cols = lax.optimization_barrier((part, other_cols))

    across = lambda p: lax.ppermute(p, VEC, [(i, i ^ 1) for i in holders])
    outer = [part] + [
        lax.ppermute(part, (ROW, VEC), [(r * n_vec + i, (r ^ q) * n_vec + i) for r in range(n_row) for i in holders])
        for q in range(1, n_row)
    ]
    count = n_vec * own_cols // 2
    parts = sum(halves, [])
    rotated, peak = call(
        functools.partial(rotate_kernel, places), flags, [filtered, shared, *parts],
        [((2 * rows, count), f32), ((8, count), f32)], [], 1 << 36,
    )
    outer, rotated, peak = lax.optimization_barrier((outer, rotated, peak))
    inner = across(jnp.concatenate(outer, axis=0))

    def solve(which):
        solved, = call(
            functools.partial(solve_kernel, places[which]), flags, [panel_inverse, *outer, inner, *halves[which]],
            [((4 * width, count // 2), bf16)],
            [pltpu.VMEM(cross.shape, bf16), pltpu.VMEM((2 * width, count // 2), f32)],
        )
        return solved

    def correct(which, solved):
        return call(
            functools.partial(correct_kernel, depth, which), flags, [rotated, peak, cols, other_cols, solved],
            [((2 * rows, count // 2), f32), ((8, count // 2), f32)], [],
        )

    piece = lambda values, i: values[:, i * own_cols : (i + 1) * own_cols]
    values, _ = correct(0, solve(0))
    values = [piece(values, j).astype(jnp.float16) for j in range(cut)]
    values, panel_inverse = lax.optimization_barrier((values, panel_inverse))
    far = {2 * (cut + j): [swapped(values[j], VEC, 2 * (cut + j))] for j in range(cut)}
    values, power = correct(1, solve(1))
    near = {}
    for j in range(1, cut):
        value = piece(values, j).astype(jnp.float16)
        near[2 * j] = [swapped(v, VEC, 2 * j) for v in (value[:rows], value[rows:])]
    near[0] = [piece(values, 0)]

    shape = jax.ShapeDtypeStruct((n_vec * rows, own_cols), f32)
    spec = lambda space: pl.BlockSpec(memory_space=space)

    def place(blocks, out):
        parts = sum(blocks.values(), [])
        return pl.pallas_call(
            functools.partial(place_kernel, [(k, len(v)) for k, v in blocks.items()]),
            in_specs=[spec(pltpu.SMEM)] + [spec(pltpu.VMEM)] * (1 + len(parts)) + [spec(pl.ANY)] * len(out),
            out_specs=spec(pl.ANY), out_shape=shape,
            scratch_shapes=[
                pltpu.VMEM((len(blocks), 2 * rows, own_cols), f32), pltpu.SemaphoreType.DMA((len(blocks),))
            ],
            input_output_aliases={2 + len(parts): 0} if out else {},
            compiler_params=pltpu.CompilerParams(vmem_limit_bytes=VMEM_LIMIT),
            cost_estimate=pl.CostEstimate(flops=1, bytes_accessed=1, transcendentals=0),
        )(flags, power, *(v.astype(f32) for v in parts), *out)

    return place(far, [place(near, [])])


def solution(mesh):
    in_specs = (P((ROW, VEC), None), P(ROW, VEC), P((ROW, VEC), None), P())
    return jax.shard_map(on_device, mesh=mesh, in_specs=in_specs, out_specs=P(ROW, VEC), check_vma=False)
```

```python
import functools

import jax
import jax.numpy as jnp
from jax import lax
from jax.experimental import pallas as pl
from jax.experimental.pallas import tpu as pltpu
from jax.sharding import PartitionSpec as P

ROW, VEC = "row", "vec"
VMEM_LIMIT = 16 * 1024 * 1024


def swapped(value, axis, offset):
    return lax.ppermute(value, axis, [(i, i ^ offset) for i in range(lax.axis_size(axis))])


def steps_of(size):
    return [1 << i for i in range(size.bit_length() - 1)]


def split(value):
    high = value.astype(jnp.bfloat16)
    return high, (value - high.astype(jnp.float32)).astype(jnp.bfloat16)


def split_array(value):
    high = lax.reduce_precision(value, 8, 7)
    return high.astype(jnp.bfloat16), (value - high).astype(jnp.bfloat16)


def mul(a, b):
    return jnp.dot(a, b, preferred_element_type=jnp.float32)


def mul3(a, b):
    left = jnp.concatenate([a[0], a[0], a[1]], axis=1)
    return mul(left, jnp.concatenate([b[0], b[1], b[0]], axis=0))


def side_kernel(order, parts, first, second):
    cut, width = len(order) // 2, parts.shape[2]
    for i, j in enumerate(order):
        (first, second)[i // cut][:, i % cut * width : (i % cut + 1) * width] = parts[j]


def gathered(parts, places, block):
    each = parts[0].shape[0] // block
    where = {q: (parts[j // each], j % each) for j, q in enumerate(places)}
    return jnp.concatenate([p[i * block : (i + 1) * block, :] for p, i in (where[q] for q in sorted(where))], axis=0)


def rotate_kernel(places, flags, own, other, *refs):
    *parts, out, peak = refs
    n_row, each, rows = len(places[0]), len(parts) // 2, own.shape[0]
    block = own.shape[1] // n_row
    for i, order in enumerate(places):
        ritz = gathered(parts[i * each : (i + 1) * each], order, block)
        where = slice(i * ritz.shape[1], (i + 1) * ritz.shape[1])
        for filtered, core in ((own, flags[1]), (other, 1 - flags[1])):
            left = jnp.concatenate(
                [filtered[:, pl.ds(pl.multiple_of((flags[2] ^ q) * block, block), block)] for q in range(n_row)], axis=1
            )
            out[pl.ds(pl.multiple_of(core * rows, rows), rows), where] = mul(left, ritz)
        most = jnp.max(jnp.abs(ritz.astype(jnp.float32)), axis=0, keepdims=True)
        peak[:, where] = jnp.broadcast_to(most, (peak.shape[0], most.shape[1]))


def solve_kernel(places, flags, inverse, *refs):
    n_row = len(places)
    here, there, parts, (out, cross, solved) = refs[0], refs[1], refs[2:-3], refs[-3:]
    size = 2 * here.shape[0] // n_row
    width = inverse.shape[1]
    block = here.shape[1]
    cross_rows = cross.shape[0] // n_row

    def tail(sent):
        rows = jnp.concatenate([t[start : start + 2 * width, :] for t, start in sent], axis=1)
        for q in range(n_row):
            start = pl.multiple_of((flags[2] ^ q) * cross_rows, cross_rows)
            t, first = sent[q]
            cross[pl.ds(start, cross_rows), :] = t[first + 2 * width : first + size, :]
        solved[...] = mul(rows, gathered(parts, places, block))

    def pieces(first, second):
        return [((first, second)[2 * q // n_row], q % (n_row // 2) * size) for q in range(n_row)]

    pl.when(flags[1] == 1)(lambda: tail(pieces(here, there)))
    pl.when(flags[1] == 0)(lambda: tail(pieces(there, here)))
    if block == 2 * width:
        between = cross[:, :width], cross[:, width:]
    else:
        between = cross[:width, :], cross[width:, :]
    last = mul3(split(inverse[1]), split(solved[width:, :]))
    middle = solved[:width, :] - mul3(between, split(last))
    after = mul3(split(inverse[0]), split(middle))
    out[width : 2 * width, :], out[3 * width :, :] = split(last)
    out[:width, :], out[2 * width : 3 * width, :] = split(after)


def correct_kernel(depth, which, flags, rotated, peak, own, other, solved, out, power):
    rows, size = own.shape[0], own.shape[1] // 2
    half = out.shape[1]
    where = slice(which * half, (which + 1) * half)
    panels = solved[:size, :].astype(jnp.float32) + solved[size:, :].astype(jnp.float32)
    bound = 8.0 * depth * peak[0:1, where] + size * jnp.max(jnp.abs(panels), axis=0, keepdims=True)
    exponent = 14.0 - jnp.floor(jnp.log2(jnp.maximum(bound, 1e-30)))
    scale = jnp.exp2(exponent)
    power[...] = jnp.broadcast_to(jnp.exp2(-exponent), power.shape)
    right = jnp.concatenate([solved[...], solved[:size, :]], axis=0)
    for cols, core in ((own, flags[1]), (other, 1 - flags[1])):
        at = pl.ds(pl.multiple_of(core * rows, rows), rows)
        left = jnp.concatenate([cols[:, :size], cols[...]], axis=1)
        out[at, :] = (rotated[at, where] - mul(left, right)) * scale

    @pl.when(flags[0] == 1)
    def _():
        out[2 * rows - size :, :] = panels * scale


def place_kernel(ks, flags, power, *refs):
    out, ready, sems = refs[-3:]
    size, width = ready.shape[1:]
    parts = list(refs)
    copies = []
    for i, (k, count) in enumerate(ks):
        for j in range(count):
            part = parts.pop(0)
            step = part.shape[0]
            ready[i, j * step : (j + 1) * step, :] = part[...] * power[0:1, :width]
        into = out.at[pl.ds(pl.multiple_of(((flags[3] ^ k) >> 1) * size, size), size), :]
        copies.append(pltpu.make_async_copy(ready.at[i], into, sems.at[i]))
        copies[i].start()
    for copy in copies:
        copy.wait()


def call(kernel, flags, inputs, out_shape, scratch, work=1):
    spec = lambda space: pl.BlockSpec(memory_space=space)
    specs, arrays, scalars = [], [], [] if flags is None else [flags]
    for value in inputs:
        group = value if isinstance(value, list) else [value]
        specs += [spec(pltpu.HBM if isinstance(value, list) else pltpu.VMEM)] * len(group)
        arrays += group
    return pl.pallas_call(
        kernel,
        in_specs=[spec(pltpu.SMEM)] * len(scalars) + specs,
        out_specs=[spec(pltpu.VMEM)] * len(out_shape),
        out_shape=[jax.ShapeDtypeStruct(*s) for s in out_shape],
        scratch_shapes=scratch,
        compiler_params=pltpu.CompilerParams(vmem_limit_bytes=VMEM_LIMIT),
        cost_estimate=pl.CostEstimate(flops=work, bytes_accessed=1, transcendentals=0),
    )(*scalars, *arrays)


def on_device(filtered, ritz, panel_cols, panel_inverse):
    rows, depth = filtered.shape
    width = panel_inverse.shape[1]
    n_row, n_vec = lax.axis_size(ROW), lax.axis_size(VEC)
    row, vec = lax.axis_index(ROW), lax.axis_index(VEC)
    block, own_cols = ritz.shape
    is_last = (row == n_row - 1) & (vec == n_vec - 1)
    last = n_row * n_vec - 1
    lower = rows - 2 * width
    cut = n_vec // 4
    f32, bf16 = jnp.float32, jnp.bfloat16
    holders = range(1, n_vec, 2)

    last_chip = (row == n_row - 1) & (vec >= n_vec - 2)
    flags = jnp.stack([last_chip.astype(jnp.int32), vec & 1, row, vec])
    filtered, ritz, panel_cols, flags, is_last = lax.optimization_barrier((filtered, ritz, panel_cols, flags, is_last))

    cross = jnp.concatenate(split_array(panel_cols[lower : lower + width, width:]), axis=1 if block == 2 * width else 0)
    cross_rows = cross.shape[0] // n_row
    def part_of(r):
        return jnp.concatenate(
            [filtered[lower:, r * block : (r + 1) * block], cross[r * cross_rows : (r + 1) * cross_rows]], axis=0
        )
    own, evens = ritz[None], [0]
    for step in steps_of(n_vec)[:0:-1]:
        own = jnp.concatenate([own, swapped(own, VEC, step)])
        evens += [k ^ step for k in evens]
    shared = swapped(filtered, VEC, 1)
    parts = [lax.ppermute(part_of(r), (ROW, VEC), [(last, r * n_vec + n_vec - 1)]) for r in range(n_row - 1)]
    part = sum(parts, jnp.where(is_last, part_of(n_row - 1), jnp.zeros((), bf16)))
    cols = jnp.concatenate(split_array(panel_cols), axis=1)
    own, part, shared, cols = lax.optimization_barrier((own, part, shared, cols))

    order = [evens.index(2 * ((cut + i) % (2 * cut))) for i in range(2 * cut)]
    halves = call(
        functools.partial(side_kernel, order), None, [own], [((block, cut * own_cols), bf16)] * 2, []
    )
    halves, places = [[h] for h in halves], [[0], [0]]
    steps, downs, sources = steps_of(n_row), steps_of(n_vec)[:0:-1], [n_vec - 1]
    for i in range(max(len(steps), len(downs))):
        if i < len(steps):
            for which, step in enumerate((steps[i], steps[-1 - i])):
                known = jnp.concatenate(halves[which], axis=0)
                halves[which] = [known, swapped(known, ROW, step)]
                places[which] = places[which] + [q ^ step for q in places[which]]
        if i < len(downs):
            part += lax.ppermute(part, VEC, [(v, v ^ downs[i]) for v in sources])
            sources += [v ^ downs[i] for v in sources]
        if i == 0:
            halves, part, cols = lax.optimization_barrier((halves, part, cols))
            other_cols = swapped(cols, VEC, 1)
    part, other_cols = lax.optimization_barrier((part, other_cols))

    pieces = [part]
    for q in range(1, n_row):
        to = 0 if q < n_row // 2 else 1
        pairs = [(r * n_vec + i, (r ^ q) * n_vec + (i ^ to)) for r in range(n_row) for i in holders]
        pieces.append(lax.ppermute(part, (ROW, VEC), pairs))
    count = n_vec * own_cols // 2
    parts = sum(halves, [])
    rotated, peak = call(
        functools.partial(rotate_kernel, places), flags, [filtered, shared, *parts],
        [((2 * rows, count), f32), ((8, count), f32)], [], 1 << 36,
    )
    pieces, rotated, peak = lax.optimization_barrier((pieces, rotated, peak))
    here = jnp.concatenate([pieces[q] + pieces[q + n_row // 2] for q in range(n_row // 2)], axis=0)
    tails = [here, swapped(here, VEC, 1)]

    def solve(which):
        solved, = call(
            functools.partial(solve_kernel, places[which]), flags, [panel_inverse, *tails, *halves[which]],
            [((4 * width, count // 2), bf16)],
            [pltpu.VMEM(cross.shape, bf16), pltpu.VMEM((2 * width, count // 2), f32)],
        )
        return solved

    def correct(which, solved):
        return call(
            functools.partial(correct_kernel, depth, which), flags, [rotated, peak, cols, other_cols, solved],
            [((2 * rows, count // 2), f32), ((8, count // 2), f32)], [],
        )

    piece = lambda values, i: values[:, i * own_cols : (i + 1) * own_cols]
    values, _ = correct(0, solve(0))
    values = [piece(values, j).astype(jnp.float16) for j in range(cut)]
    values, panel_inverse = lax.optimization_barrier((values, panel_inverse))
    far = {2 * (cut + j): [swapped(values[j], VEC, 2 * (cut + j))] for j in range(cut)}
    values, power = correct(1, solve(1))
    near = {}
    for j in range(1, cut):
        value = piece(values, j).astype(jnp.float16)
        near[2 * j] = [swapped(v, VEC, 2 * j) for v in (value[:rows], value[rows:])]
    near[0] = [piece(values, 0)]

    shape = jax.ShapeDtypeStruct((n_vec * rows, own_cols), f32)
    spec = lambda space: pl.BlockSpec(memory_space=space)

    def place(blocks, out):
        parts = sum(blocks.values(), [])
        return pl.pallas_call(
            functools.partial(place_kernel, [(k, len(v)) for k, v in blocks.items()]),
            in_specs=[spec(pltpu.SMEM)] + [spec(pltpu.VMEM)] * (1 + len(parts)) + [spec(pl.ANY)] * len(out),
            out_specs=spec(pl.ANY), out_shape=shape,
            scratch_shapes=[
                pltpu.VMEM((len(blocks), 2 * rows, own_cols), f32), pltpu.SemaphoreType.DMA((len(blocks),))
            ],
            input_output_aliases={2 + len(parts): 0} if out else {},
            compiler_params=pltpu.CompilerParams(vmem_limit_bytes=VMEM_LIMIT),
            cost_estimate=pl.CostEstimate(flops=1, bytes_accessed=1, transcendentals=0),
        )(flags, power, *(v.astype(f32) for v in parts), *out)

    return place(far, [place(near, [])])


def solution(mesh):
    in_specs = (P((ROW, VEC), None), P(ROW, VEC), P((ROW, VEC), None), P())
    return jax.shard_map(on_device, mesh=mesh, in_specs=in_specs, out_specs=P(ROW, VEC), check_vma=False)
```

```python
import functools

import jax
import jax.numpy as jnp
from jax import lax
from jax.experimental import pallas as pl
from jax.experimental.pallas import tpu as pltpu
from jax.sharding import PartitionSpec as P

ROW, VEC = "row", "vec"
VMEM_LIMIT = 16 * 1024 * 1024


def swapped(value, axis, offset):
    return lax.ppermute(value, axis, [(i, i ^ offset) for i in range(lax.axis_size(axis))])


def steps_of(size):
    return [1 << i for i in range(size.bit_length() - 1)]


def split(value):
    high = value.astype(jnp.bfloat16)
    return high, (value - high.astype(jnp.float32)).astype(jnp.bfloat16)


def split_array(value):
    high = lax.reduce_precision(value, 8, 7)
    return high.astype(jnp.bfloat16), (value - high).astype(jnp.bfloat16)


def mul(a, b):
    return jnp.dot(a, b, preferred_element_type=jnp.float32)


def mul3(a, b):
    left = jnp.concatenate([a[0], a[0], a[1]], axis=1)
    return mul(left, jnp.concatenate([b[0], b[1], b[0]], axis=0))


def side_kernel(order, parts, first, second):
    cut, width = len(order) // 2, parts.shape[2]
    for i, j in enumerate(order):
        (first, second)[i // cut][:, i % cut * width : (i % cut + 1) * width] = parts[j]


def gathered(parts, places, block):
    each = parts[0].shape[0] // block
    where = {q: (parts[j // each], j % each) for j, q in enumerate(places)}
    return jnp.concatenate([p[i * block : (i + 1) * block, :] for p, i in (where[q] for q in sorted(where))], axis=0)


def rotate_kernel(places, flags, own, other, *refs):
    *parts, out, peak = refs
    n_row, each, rows = len(places[0]), len(parts) // 2, own.shape[0]
    block = own.shape[1] // n_row
    for i, order in enumerate(places):
        ritz = gathered(parts[i * each : (i + 1) * each], order, block)
        where = slice(i * ritz.shape[1], (i + 1) * ritz.shape[1])
        for filtered, core in ((own, flags[1]), (other, 1 - flags[1])):
            left = jnp.concatenate(
                [filtered[:, pl.ds(pl.multiple_of((flags[2] ^ q) * block, block), block)] for q in range(n_row)], axis=1
            )
            out[pl.ds(pl.multiple_of(core * rows, rows), rows), where] = mul(left, ritz)
        most = jnp.max(jnp.abs(ritz.astype(jnp.float32)), axis=0, keepdims=True)
        peak[:, where] = jnp.broadcast_to(most, (peak.shape[0], most.shape[1]))


def solve_kernel(places, flags, inverse, *refs):
    n_row = len(places)
    here, there, parts, (out, cross, solved) = refs[0], refs[1], refs[2:-3], refs[-3:]
    size = 2 * here.shape[0] // n_row
    width = inverse.shape[1]
    block = here.shape[1]
    cross_rows = cross.shape[0] // n_row

    def tail(sent):
        rows = jnp.concatenate([t[start : start + 2 * width, :] for t, start in sent], axis=1)
        for q in range(n_row):
            start = pl.multiple_of((flags[2] ^ q) * cross_rows, cross_rows)
            t, first = sent[q]
            cross[pl.ds(start, cross_rows), :] = t[first + 2 * width : first + size, :]
        solved[...] = mul(rows, gathered(parts, places, block))

    def pieces(first, second):
        return [((first, second)[2 * q // n_row], q % (n_row // 2) * size) for q in range(n_row)]

    pl.when(flags[1] == 1)(lambda: tail(pieces(here, there)))
    pl.when(flags[1] == 0)(lambda: tail(pieces(there, here)))
    if block == 2 * width:
        between = cross[:, :width], cross[:, width:]
    else:
        between = cross[:width, :], cross[width:, :]
    last = mul3(split(inverse[1]), split(solved[width:, :]))
    middle = solved[:width, :] - mul3(between, split(last))
    after = mul3(split(inverse[0]), split(middle))
    out[width : 2 * width, :], out[3 * width :, :] = split(last)
    out[:width, :], out[2 * width : 3 * width, :] = split(after)


def correct_kernel(depth, which, flags, rotated, peak, own, other, solved, out, power):
    rows, size = own.shape[0], own.shape[1] // 2
    half = out.shape[1]
    where = slice(which * half, (which + 1) * half)
    panels = solved[:size, :].astype(jnp.float32) + solved[size:, :].astype(jnp.float32)
    bound = 8.0 * depth * peak[0:1, where] + size * jnp.max(jnp.abs(panels), axis=0, keepdims=True)
    exponent = 14.0 - jnp.floor(jnp.log2(jnp.maximum(bound, 1e-30)))
    scale = jnp.exp2(exponent)
    power[...] = jnp.broadcast_to(jnp.exp2(-exponent), power.shape)
    right = jnp.concatenate([solved[...], solved[:size, :]], axis=0)
    for cols, core in ((own, flags[1]), (other, 1 - flags[1])):
        at = pl.ds(pl.multiple_of(core * rows, rows), rows)
        left = jnp.concatenate([cols[:, :size], cols[...]], axis=1)
        out[at, :] = (rotated[at, where] - mul(left, right)) * scale

    @pl.when(flags[0] == 1)
    def _():
        out[2 * rows - size :, :] = panels * scale


def place_kernel(ks, flags, power, *refs):
    out, ready, sems = refs[-3:]
    size, width = ready.shape[1:]
    parts = list(refs)
    copies = []
    for i, (k, count) in enumerate(ks):
        for j in range(count):
            part = parts.pop(0)
            step = part.shape[0]
            ready[i, j * step : (j + 1) * step, :] = part[...] * power[0:1, :width]
        into = out.at[pl.ds(pl.multiple_of(((flags[3] ^ k) >> 1) * size, size), size), :]
        copies.append(pltpu.make_async_copy(ready.at[i], into, sems.at[i]))
        copies[i].start()
    for copy in copies:
        copy.wait()


def call(kernel, flags, inputs, out_shape, scratch, work=1):
    spec = lambda space: pl.BlockSpec(memory_space=space)
    specs, arrays, scalars = [], [], [] if flags is None else [flags]
    for value in inputs:
        group = value if isinstance(value, list) else [value]
        specs += [spec(pltpu.HBM if isinstance(value, list) else pltpu.VMEM)] * len(group)
        arrays += group
    return pl.pallas_call(
        kernel,
        in_specs=[spec(pltpu.SMEM)] * len(scalars) + specs,
        out_specs=[spec(pltpu.VMEM)] * len(out_shape),
        out_shape=[jax.ShapeDtypeStruct(*s) for s in out_shape],
        scratch_shapes=scratch,
        compiler_params=pltpu.CompilerParams(vmem_limit_bytes=VMEM_LIMIT),
        cost_estimate=pl.CostEstimate(flops=work, bytes_accessed=1, transcendentals=0),
    )(*scalars, *arrays)


def on_device(filtered, ritz, panel_cols, panel_inverse):
    rows, depth = filtered.shape
    width = panel_inverse.shape[1]
    n_row, n_vec = lax.axis_size(ROW), lax.axis_size(VEC)
    row, vec = lax.axis_index(ROW), lax.axis_index(VEC)
    block, own_cols = ritz.shape
    is_last = (row == n_row - 1) & (vec == n_vec - 1)
    last = n_row * n_vec - 1
    lower = rows - 2 * width
    cut = n_vec // 4
    f32, bf16 = jnp.float32, jnp.bfloat16
    holders = range(1, n_vec, 2)

    last_chip = (row == n_row - 1) & (vec >= n_vec - 2)
    flags = jnp.stack([last_chip.astype(jnp.int32), vec & 1, row, vec])
    filtered, ritz, panel_cols, flags, is_last = lax.optimization_barrier((filtered, ritz, panel_cols, flags, is_last))

    cross = jnp.concatenate(split_array(panel_cols[lower : lower + width, width:]), axis=1 if block == 2 * width else 0)
    cross_rows = cross.shape[0] // n_row
    def part_of(r):
        return jnp.concatenate(
            [filtered[lower:, r * block : (r + 1) * block], cross[r * cross_rows : (r + 1) * cross_rows]], axis=0
        )
    own, evens = ritz[None], [0]
    for step in steps_of(n_vec)[:0:-1]:
        own = jnp.concatenate([own, swapped(own, VEC, step)])
        evens += [k ^ step for k in evens]
    shared = swapped(filtered, VEC, 1)
    parts = [lax.ppermute(part_of(r), (ROW, VEC), [(last, r * n_vec + n_vec - 1)]) for r in range(n_row - 1)]
    part = sum(parts, jnp.where(is_last, part_of(n_row - 1), jnp.zeros((), bf16)))
    cols = jnp.concatenate(split_array(panel_cols), axis=1)
    own, part, shared, cols = lax.optimization_barrier((own, part, shared, cols))

    order = [evens.index(2 * ((cut + i) % (2 * cut))) for i in range(2 * cut)]
    halves = call(
        functools.partial(side_kernel, order), None, [own], [((block, cut * own_cols), bf16)] * 2, []
    )
    halves, places = [[h] for h in halves], [[0], [0]]
    steps, downs, sources = steps_of(n_row), steps_of(n_vec)[:0:-1], [n_vec - 1]
    for i in range(max(len(steps), len(downs))):
        if i < len(steps):
            for which, step in enumerate((steps[i], steps[-1 - i])):
                known = jnp.concatenate(halves[which], axis=0)
                halves[which] = [known, swapped(known, ROW, step)]
                places[which] = places[which] + [q ^ step for q in places[which]]
        if i < len(downs):
            part += lax.ppermute(part, VEC, [(v, v ^ downs[i]) for v in sources])
            sources += [v ^ downs[i] for v in sources]
        if i == 0:
            halves, part, cols = lax.optimization_barrier((halves, part, cols))
            other_cols = swapped(cols, VEC, 1)
    part, other_cols = lax.optimization_barrier((part, other_cols))

    pieces = [part]
    for q in range(1, n_row):
        to = 0 if q < n_row // 2 else 1
        pairs = [(r * n_vec + i, (r ^ q) * n_vec + (i ^ to)) for r in range(n_row) for i in holders]
        pieces.append(lax.ppermute(part, (ROW, VEC), pairs))
    count = n_vec * own_cols // 2
    parts = sum(halves, [])
    rotated, peak = call(
        functools.partial(rotate_kernel, places), flags, [filtered, shared, *parts],
        [((2 * rows, count), f32), ((8, count), f32)], [], 4 * rows * depth * count,
    )
    pieces, rotated, peak = lax.optimization_barrier((pieces, rotated, peak))
    here = jnp.concatenate([pieces[q] + pieces[q + n_row // 2] for q in range(n_row // 2)], axis=0)
    tails = [here, swapped(here, VEC, 1)]

    def solve(which):
        solved, = call(
            functools.partial(solve_kernel, places[which]), flags, [panel_inverse, *tails, *halves[which]],
            [((4 * width, count // 2), bf16)],
            [pltpu.VMEM(cross.shape, bf16), pltpu.VMEM((2 * width, count // 2), f32)],
        )
        return solved

    def correct(which, solved):
        return call(
            functools.partial(correct_kernel, depth, which), flags, [rotated, peak, cols, other_cols, solved],
            [((2 * rows, count // 2), f32), ((8, count // 2), f32)], [],
        )

    piece = lambda values, i: values[:, i * own_cols : (i + 1) * own_cols]
    values, _ = correct(0, solve(0))
    values = [piece(values, j).astype(jnp.float16) for j in range(cut)]
    values, panel_inverse = lax.optimization_barrier((values, panel_inverse))
    far = {2 * (cut + j): [swapped(values[j], VEC, 2 * (cut + j))] for j in range(cut)}
    values, power = correct(1, solve(1))
    near = {}
    for j in range(1, cut):
        value = piece(values, j).astype(jnp.float16)
        near[2 * j] = [swapped(v, VEC, 2 * j) for v in (value[:rows], value[rows:])]
    near[0] = [piece(values, 0)]

    shape = jax.ShapeDtypeStruct((n_vec * rows, own_cols), f32)
    spec = lambda space: pl.BlockSpec(memory_space=space)

    def place(blocks, out):
        parts = sum(blocks.values(), [])
        return pl.pallas_call(
            functools.partial(place_kernel, [(k, len(v)) for k, v in blocks.items()]),
            in_specs=[spec(pltpu.SMEM)] + [spec(pltpu.VMEM)] * (1 + len(parts)) + [spec(pl.ANY)] * len(out),
            out_specs=spec(pl.ANY), out_shape=shape,
            scratch_shapes=[
                pltpu.VMEM((len(blocks), 2 * rows, own_cols), f32), pltpu.SemaphoreType.DMA((len(blocks),))
            ],
            input_output_aliases={2 + len(parts): 0} if out else {},
            compiler_params=pltpu.CompilerParams(vmem_limit_bytes=VMEM_LIMIT),
            cost_estimate=pl.CostEstimate(flops=1, bytes_accessed=1, transcendentals=0),
        )(flags, power, *(v.astype(f32) for v in parts), *out)

    return place(far, [place(near, [])])


def solution(mesh):
    in_specs = (P((ROW, VEC), None), P(ROW, VEC), P((ROW, VEC), None), P())
    return jax.shard_map(on_device, mesh=mesh, in_specs=in_specs, out_specs=P(ROW, VEC), check_vma=False)
```

```python
import functools

import jax
import jax.numpy as jnp
from jax import lax
from jax.experimental import pallas as pl
from jax.experimental.pallas import tpu as pltpu
from jax.sharding import PartitionSpec as P

ROW, VEC = "row", "vec"
VMEM_LIMIT = 16 * 1024 * 1024


def swapped(value, axis, offset):
    return lax.ppermute(value, axis, [(i, i ^ offset) for i in range(lax.axis_size(axis))])


def steps_of(size):
    return [1 << i for i in range(size.bit_length() - 1)]


def split(value):
    high = value.astype(jnp.bfloat16)
    return high, (value - high.astype(jnp.float32)).astype(jnp.bfloat16)


def split_array(value):
    high = lax.reduce_precision(value, 8, 7)
    return high.astype(jnp.bfloat16), (value - high).astype(jnp.bfloat16)


def mul(a, b):
    return jnp.dot(a, b, preferred_element_type=jnp.float32)


def mul3(a, b):
    left = jnp.concatenate([a[0], a[0], a[1]], axis=1)
    return mul(left, jnp.concatenate([b[0], b[1], b[0]], axis=0))


def side_kernel(order, parts, first, second):
    cut, width = len(order) // 2, parts.shape[2]
    for i, j in enumerate(order):
        (first, second)[i // cut][:, i % cut * width : (i % cut + 1) * width] = parts[j]


def gathered(parts, places, block):
    each = parts[0].shape[0] // block
    where = {q: (parts[j // each], j % each) for j, q in enumerate(places)}
    return jnp.concatenate([p[i * block : (i + 1) * block, :] for p, i in (where[q] for q in sorted(where))], axis=0)


def rotate_kernel(places, flags, own, other, *refs):
    *parts, out, peak = refs
    n_row, each, rows = len(places[0]), len(parts) // 2, own.shape[0]
    block = own.shape[1] // n_row
    for i, order in enumerate(places):
        ritz = gathered(parts[i * each : (i + 1) * each], order, block)
        where = slice(i * ritz.shape[1], (i + 1) * ritz.shape[1])
        for filtered, core in ((own, flags[1]), (other, 1 - flags[1])):
            left = jnp.concatenate(
                [filtered[:, pl.ds(pl.multiple_of((flags[2] ^ q) * block, block), block)] for q in range(n_row)], axis=1
            )
            out[pl.ds(pl.multiple_of(core * rows, rows), rows), where] = mul(left, ritz)
        most = jnp.max(jnp.abs(ritz.astype(jnp.float32)), axis=0, keepdims=True)
        peak[:, where] = jnp.broadcast_to(most, (peak.shape[0], most.shape[1]))


def solve_kernel(places, flags, inverse, *refs):
    n_row = len(places)
    here, there, parts, (out, cross, solved) = refs[0], refs[1], refs[2:-3], refs[-3:]
    size = 2 * here.shape[0] // n_row
    width = inverse.shape[1]
    block = here.shape[1]
    cross_rows = cross.shape[0] // n_row

    def tail(sent):
        rows = jnp.concatenate([t[start : start + 2 * width, :] for t, start in sent], axis=1)
        for q in range(n_row):
            start = pl.multiple_of((flags[2] ^ q) * cross_rows, cross_rows)
            t, first = sent[q]
            cross[pl.ds(start, cross_rows), :] = t[first + 2 * width : first + size, :]
        solved[...] = mul(rows, gathered(parts, places, block))

    def pieces(first, second):
        return [((first, second)[2 * q // n_row], q % (n_row // 2) * size) for q in range(n_row)]

    pl.when(flags[1] == 1)(lambda: tail(pieces(here, there)))
    pl.when(flags[1] == 0)(lambda: tail(pieces(there, here)))
    if block == 2 * width:
        between = cross[:, :width], cross[:, width:]
    else:
        between = cross[:width, :], cross[width:, :]
    last = mul3(split(inverse[1]), split(solved[width:, :]))
    middle = solved[:width, :] - mul3(between, split(last))
    after = mul3(split(inverse[0]), split(middle))
    out[width : 2 * width, :], out[3 * width :, :] = split(last)
    out[:width, :], out[2 * width : 3 * width, :] = split(after)


def correct_kernel(depth, which, flags, rotated, peak, own, other, solved, out, power):
    rows, size = own.shape[0], own.shape[1] // 2
    half = out.shape[1]
    where = slice(which * half, (which + 1) * half)
    panels = solved[:size, :].astype(jnp.float32) + solved[size:, :].astype(jnp.float32)
    bound = 8.0 * depth * peak[0:1, where] + size * jnp.max(jnp.abs(panels), axis=0, keepdims=True)
    exponent = 14.0 - jnp.floor(jnp.log2(jnp.maximum(bound, 1e-30)))
    scale = jnp.exp2(exponent)
    power[...] = jnp.broadcast_to(jnp.exp2(-exponent), power.shape)
    right = jnp.concatenate([solved[...], solved[:size, :]], axis=0)
    for cols, core in ((own, flags[1]), (other, 1 - flags[1])):
        at = pl.ds(pl.multiple_of(core * rows, rows), rows)
        left = jnp.concatenate([cols[:, :size], cols[...]], axis=1)
        out[at, :] = (rotated[at, where] - mul(left, right)) * scale

    @pl.when(flags[0] == 1)
    def _():
        out[2 * rows - size :, :] = panels * scale


def finish_kernel(places, depth, which, flags, inverse, here, there, *refs):
    *parts, rotated, peak, own, other, out, power, terms, cross, solved = refs
    solve_kernel(places, flags, inverse, here, there, *parts, terms, cross, solved)
    correct_kernel(depth, which, flags, rotated, peak, own, other, terms, out, power)


def place_kernel(ks, flags, power, *refs):
    out, ready, sems = refs[-3:]
    size, width = ready.shape[1:]
    parts = list(refs)
    copies = []
    for i, (k, count) in enumerate(ks):
        for j in range(count):
            part = parts.pop(0)
            step = part.shape[0]
            ready[i, j * step : (j + 1) * step, :] = part[...] * power[0:1, :width]
        into = out.at[pl.ds(pl.multiple_of(((flags[3] ^ k) >> 1) * size, size), size), :]
        copies.append(pltpu.make_async_copy(ready.at[i], into, sems.at[i]))
        copies[i].start()
    for copy in copies:
        copy.wait()


def call(kernel, flags, inputs, out_shape, scratch, work=1):
    spec = lambda space: pl.BlockSpec(memory_space=space)
    specs, arrays, scalars = [], [], [] if flags is None else [flags]
    for value in inputs:
        group = value if isinstance(value, list) else [value]
        specs += [spec(pltpu.HBM if isinstance(value, list) else pltpu.VMEM)] * len(group)
        arrays += group
    return pl.pallas_call(
        kernel,
        in_specs=[spec(pltpu.SMEM)] * len(scalars) + specs,
        out_specs=[spec(pltpu.VMEM)] * len(out_shape),
        out_shape=[jax.ShapeDtypeStruct(*s) for s in out_shape],
        scratch_shapes=scratch,
        compiler_params=pltpu.CompilerParams(vmem_limit_bytes=VMEM_LIMIT),
        cost_estimate=pl.CostEstimate(flops=work, bytes_accessed=1, transcendentals=0),
    )(*scalars, *arrays)


def on_device(filtered, ritz, panel_cols, panel_inverse):
    rows, depth = filtered.shape
    width = panel_inverse.shape[1]
    n_row, n_vec = lax.axis_size(ROW), lax.axis_size(VEC)
    row, vec = lax.axis_index(ROW), lax.axis_index(VEC)
    block, own_cols = ritz.shape
    is_last = (row == n_row - 1) & (vec == n_vec - 1)
    last = n_row * n_vec - 1
    lower = rows - 2 * width
    cut = n_vec // 4
    f32, bf16 = jnp.float32, jnp.bfloat16
    holders = range(1, n_vec, 2)

    last_chip = (row == n_row - 1) & (vec >= n_vec - 2)
    flags = jnp.stack([last_chip.astype(jnp.int32), vec & 1, row, vec])
    filtered, ritz, panel_cols, flags, is_last = lax.optimization_barrier((filtered, ritz, panel_cols, flags, is_last))

    cross = jnp.concatenate(split_array(panel_cols[lower : lower + width, width:]), axis=1 if block == 2 * width else 0)
    cross_rows = cross.shape[0] // n_row
    def part_of(r):
        return jnp.concatenate(
            [filtered[lower:, r * block : (r + 1) * block], cross[r * cross_rows : (r + 1) * cross_rows]], axis=0
        )
    own, evens = ritz[None], [0]
    for step in steps_of(n_vec)[:0:-1]:
        own = jnp.concatenate([own, swapped(own, VEC, step)])
        evens += [k ^ step for k in evens]
    shared = swapped(filtered, VEC, 1)
    parts = [lax.ppermute(part_of(r), (ROW, VEC), [(last, r * n_vec + n_vec - 1)]) for r in range(n_row - 1)]
    part = sum(parts, jnp.where(is_last, part_of(n_row - 1), jnp.zeros((), bf16)))
    cols = jnp.concatenate(split_array(panel_cols), axis=1)
    own, part, shared, cols = lax.optimization_barrier((own, part, shared, cols))

    order = [evens.index(2 * ((cut + i) % (2 * cut))) for i in range(2 * cut)]
    halves = call(
        functools.partial(side_kernel, order), None, [own], [((block, cut * own_cols), bf16)] * 2, []
    )
    halves, places = [[h] for h in halves], [[0], [0]]
    steps, downs, sources = steps_of(n_row), steps_of(n_vec)[:0:-1], [n_vec - 1]
    for i in range(max(len(steps), len(downs))):
        if i < len(steps):
            for which, step in enumerate((steps[-1 - i], steps[i])):
                known = jnp.concatenate(halves[which], axis=0)
                halves[which] = [known, swapped(known, ROW, step)]
                places[which] = places[which] + [q ^ step for q in places[which]]
        if i < len(downs):
            part += lax.ppermute(part, VEC, [(v, v ^ downs[i]) for v in sources])
            sources += [v ^ downs[i] for v in sources]
        if i == 0:
            halves, part, cols = lax.optimization_barrier((halves, part, cols))
            other_cols = swapped(cols, VEC, 1)
    part, other_cols = lax.optimization_barrier((part, other_cols))

    pieces = [part]
    for q in range(1, n_row):
        to = 0 if q < n_row // 2 else 1
        pairs = [(r * n_vec + i, (r ^ q) * n_vec + (i ^ to)) for r in range(n_row) for i in holders]
        pieces.append(lax.ppermute(part, (ROW, VEC), pairs))
    count = n_vec * own_cols // 2
    parts = sum(halves, [])
    rotated, peak = call(
        functools.partial(rotate_kernel, places), flags, [filtered, shared, *parts],
        [((2 * rows, count), f32), ((8, count), f32)], [], 4 * rows * depth * count,
    )
    pieces, rotated, peak = lax.optimization_barrier((pieces, rotated, peak))
    here = jnp.concatenate([pieces[q] + pieces[q + n_row // 2] for q in range(n_row // 2)], axis=0)
    tails = [here, swapped(here, VEC, 1)]

    def finish(which):
        return call(
            functools.partial(finish_kernel, places[which], depth, which), flags,
            [panel_inverse, *tails, *halves[which], rotated, peak, cols, other_cols],
            [((2 * rows, count // 2), f32), ((8, count // 2), f32)],
            [
                pltpu.VMEM((4 * width, count // 2), bf16), pltpu.VMEM(cross.shape, bf16),
                pltpu.VMEM((2 * width, count // 2), f32),
            ],
        )

    piece = lambda values, i: values[:, i * own_cols : (i + 1) * own_cols]
    values, _ = finish(0)
    values = [piece(values, j).astype(jnp.float16) for j in range(cut)]
    values, panel_inverse = lax.optimization_barrier((values, panel_inverse))
    far = {2 * (cut + j): [swapped(values[j], VEC, 2 * (cut + j))] for j in range(cut)}
    values, power = finish(1)
    near = {}
    for j in range(1, cut):
        value = piece(values, j).astype(jnp.float16)
        near[2 * j] = [swapped(v, VEC, 2 * j) for v in (value[:rows], value[rows:])]
    near[0] = [piece(values, 0)]

    shape = jax.ShapeDtypeStruct((n_vec * rows, own_cols), f32)
    spec = lambda space: pl.BlockSpec(memory_space=space)

    def place(blocks, out):
        parts = sum(blocks.values(), [])
        return pl.pallas_call(
            functools.partial(place_kernel, [(k, len(v)) for k, v in blocks.items()]),
            in_specs=[spec(pltpu.SMEM)] + [spec(pltpu.VMEM)] * (1 + len(parts)) + [spec(pl.ANY)] * len(out),
            out_specs=spec(pl.ANY), out_shape=shape,
            scratch_shapes=[
                pltpu.VMEM((len(blocks), 2 * rows, own_cols), f32), pltpu.SemaphoreType.DMA((len(blocks),))
            ],
            input_output_aliases={2 + len(parts): 0} if out else {},
            compiler_params=pltpu.CompilerParams(vmem_limit_bytes=VMEM_LIMIT),
            cost_estimate=pl.CostEstimate(flops=1, bytes_accessed=1, transcendentals=0),
        )(flags, power, *(v.astype(f32) for v in parts), *out)

    return place(far, [place(near, [])])


def solution(mesh):
    in_specs = (P((ROW, VEC), None), P(ROW, VEC), P((ROW, VEC), None), P())
    return jax.shard_map(on_device, mesh=mesh, in_specs=in_specs, out_specs=P(ROW, VEC), check_vma=False)
```

```python
import functools

import jax
import jax.numpy as jnp
from jax import lax
from jax.experimental import pallas as pl
from jax.experimental.pallas import tpu as pltpu
from jax.sharding import PartitionSpec as P

ROW, VEC = "row", "vec"
VMEM_LIMIT = 16 * 1024 * 1024


def swapped(value, axis, offset):
    return lax.ppermute(value, axis, [(i, i ^ offset) for i in range(lax.axis_size(axis))])


def steps_of(size):
    return [1 << i for i in range(size.bit_length() - 1)]


def split(value):
    high = value.astype(jnp.bfloat16)
    return high, (value - high.astype(jnp.float32)).astype(jnp.bfloat16)


def split_array(value):
    high = lax.reduce_precision(value, 8, 7)
    return high.astype(jnp.bfloat16), (value - high).astype(jnp.bfloat16)


def mul(a, b):
    return jnp.dot(a, b, preferred_element_type=jnp.float32)


def mul3(a, b):
    left = jnp.concatenate([a[0], a[0], a[1]], axis=1)
    return mul(left, jnp.concatenate([b[0], b[1], b[0]], axis=0))


def side_kernel(order, parts, first, second):
    cut, width = len(order) // 2, parts.shape[2]
    for i, j in enumerate(order):
        (first, second)[i // cut][:, i % cut * width : (i % cut + 1) * width] = parts[j]


def gathered(parts, places, block):
    each = parts[0].shape[0] // block
    where = {q: (parts[j // each], j % each) for j, q in enumerate(places)}
    return jnp.concatenate([p[i * block : (i + 1) * block, :] for p, i in (where[q] for q in sorted(where))], axis=0)


def rotate_kernel(places, flags, own, other, *refs):
    *parts, out, peak = refs
    n_row, each, rows = len(places[0]), len(parts) // 2, own.shape[0]
    block = own.shape[1] // n_row
    for i, order in enumerate(places):
        ritz = gathered(parts[i * each : (i + 1) * each], order, block)
        where = slice(i * ritz.shape[1], (i + 1) * ritz.shape[1])
        for filtered, core in ((own, flags[1]), (other, 1 - flags[1])):
            left = jnp.concatenate(
                [filtered[:, pl.ds(pl.multiple_of((flags[2] ^ q) * block, block), block)] for q in range(n_row)], axis=1
            )
            out[pl.ds(pl.multiple_of(core * rows, rows), rows), where] = mul(left, ritz)
        most = jnp.max(jnp.abs(ritz.astype(jnp.float32)), axis=0, keepdims=True)
        peak[:, where] = jnp.broadcast_to(most, (peak.shape[0], most.shape[1]))


def solve_kernel(places, flags, inverse, *refs):
    n_row = len(places)
    here, there, parts, (out, cross, solved) = refs[0], refs[1], refs[2:-3], refs[-3:]
    size = 2 * here.shape[0] // n_row
    width = inverse.shape[1]
    block = here.shape[1]
    cross_rows = cross.shape[0] // n_row

    def tail(sent):
        rows = jnp.concatenate([t[start : start + 2 * width, :] for t, start in sent], axis=1)
        for q in range(n_row):
            start = pl.multiple_of((flags[2] ^ q) * cross_rows, cross_rows)
            t, first = sent[q]
            cross[pl.ds(start, cross_rows), :] = t[first + 2 * width : first + size, :]
        solved[...] = mul(rows, gathered(parts, places, block))

    def pieces(first, second):
        return [((first, second)[2 * q // n_row], q % (n_row // 2) * size) for q in range(n_row)]

    pl.when(flags[1] == 1)(lambda: tail(pieces(here, there)))
    pl.when(flags[1] == 0)(lambda: tail(pieces(there, here)))
    if block == 2 * width:
        between = cross[:, :width], cross[:, width:]
    else:
        between = cross[:width, :], cross[width:, :]
    last = mul3(split(inverse[1]), split(solved[width:, :]))
    middle = solved[:width, :] - mul3(between, split(last))
    after = mul3(split(inverse[0]), split(middle))
    out[width : 2 * width, :], out[3 * width :, :] = split(last)
    out[:width, :], out[2 * width : 3 * width, :] = split(after)


def correct_kernel(depth, which, flags, rotated, peak, own, other, solved, out, power):
    rows, size = own.shape[0], own.shape[1] // 2
    half = out.shape[1]
    where = slice(which * half, (which + 1) * half)
    panels = solved[:size, :].astype(jnp.float32) + solved[size:, :].astype(jnp.float32)
    bound = 8.0 * depth * peak[0:1, where] + size * jnp.max(jnp.abs(panels), axis=0, keepdims=True)
    exponent = 14.0 - jnp.floor(jnp.log2(jnp.maximum(bound, 1e-30)))
    scale = jnp.exp2(exponent)
    power[...] = jnp.broadcast_to(jnp.exp2(-exponent), power.shape)
    right = jnp.concatenate([solved[...], solved[:size, :]], axis=0)
    for cols, core in ((own, flags[1]), (other, 1 - flags[1])):
        at = pl.ds(pl.multiple_of(core * rows, rows), rows)
        left = jnp.concatenate([cols[:, :size], cols[...]], axis=1)
        out[at, :] = (rotated[at, where] - mul(left, right)) * scale

    @pl.when(flags[0] == 1)
    def _():
        out[2 * rows - size :, :] = panels * scale


def finish_kernel(places, depth, which, flags, inverse, here, there, *refs):
    *parts, rotated, peak, own, other, out, power, terms, cross, solved = refs
    solve_kernel(places, flags, inverse, here, there, *parts, terms, cross, solved)
    correct_kernel(depth, which, flags, rotated, peak, own, other, terms, out, power)


def place_kernel(ks, flags, power, *refs):
    out, ready, sems = refs[-3:]
    size, width = ready.shape[1:]
    parts = list(refs)
    copies = []
    for i, (k, count) in enumerate(ks):
        for j in range(count):
            part = parts.pop(0)
            step = part.shape[0]
            ready[i, j * step : (j + 1) * step, :] = part[...] * power[0:1, :width]
        into = out.at[pl.ds(pl.multiple_of(((flags[3] ^ k) >> 1) * size, size), size), :]
        copies.append(pltpu.make_async_copy(ready.at[i], into, sems.at[i]))
        copies[i].start()
    for copy in copies:
        copy.wait()


def call(kernel, flags, inputs, out_shape, scratch, work=1):
    spec = lambda space: pl.BlockSpec(memory_space=space)
    specs, arrays, scalars = [], [], [] if flags is None else [flags]
    for value in inputs:
        group = value if isinstance(value, list) else [value]
        specs += [spec(pltpu.HBM if isinstance(value, list) else pltpu.VMEM)] * len(group)
        arrays += group
    return pl.pallas_call(
        kernel,
        in_specs=[spec(pltpu.SMEM)] * len(scalars) + specs,
        out_specs=[spec(pltpu.VMEM)] * len(out_shape),
        out_shape=[jax.ShapeDtypeStruct(*s) for s in out_shape],
        scratch_shapes=scratch,
        compiler_params=pltpu.CompilerParams(vmem_limit_bytes=VMEM_LIMIT),
        cost_estimate=pl.CostEstimate(flops=work, bytes_accessed=1, transcendentals=0),
    )(*scalars, *arrays)


def on_device(filtered, ritz, panel_cols, panel_inverse):
    rows, depth = filtered.shape
    width = panel_inverse.shape[1]
    n_row, n_vec = lax.axis_size(ROW), lax.axis_size(VEC)
    row, vec = lax.axis_index(ROW), lax.axis_index(VEC)
    block, own_cols = ritz.shape
    is_last = (row == n_row - 1) & (vec == n_vec - 1)
    last = n_row * n_vec - 1
    lower = rows - 2 * width
    cut = n_vec // 4
    f32, bf16 = jnp.float32, jnp.bfloat16
    holders = range(1, n_vec, 2)

    last_chip = (row == n_row - 1) & (vec >= n_vec - 2)
    flags = jnp.stack([last_chip.astype(jnp.int32), vec & 1, row, vec])
    filtered, ritz, panel_cols, flags, is_last = lax.optimization_barrier((filtered, ritz, panel_cols, flags, is_last))

    cross = jnp.concatenate(split_array(panel_cols[lower : lower + width, width:]), axis=1 if block == 2 * width else 0)
    cross_rows = cross.shape[0] // n_row
    def part_of(r):
        return jnp.concatenate(
            [filtered[lower:, r * block : (r + 1) * block], cross[r * cross_rows : (r + 1) * cross_rows]], axis=0
        )
    own, evens = ritz[None], [0]
    for step in steps_of(n_vec)[:0:-1]:
        own = jnp.concatenate([own, swapped(own, VEC, step)])
        evens += [k ^ step for k in evens]
    shared = swapped(filtered, VEC, 1)
    parts = [lax.ppermute(part_of(r), (ROW, VEC), [(last, r * n_vec + n_vec - 1)]) for r in range(n_row - 1)]
    part = sum(parts, jnp.where(is_last, part_of(n_row - 1), jnp.zeros((), bf16)))
    cols = jnp.concatenate(split_array(panel_cols), axis=1)
    own, part, shared, cols = lax.optimization_barrier((own, part, shared, cols))
    other_cols = swapped(cols, VEC, 1)

    order = [evens.index(2 * ((cut + i) % (2 * cut))) for i in range(2 * cut)]
    halves = call(
        functools.partial(side_kernel, order), None, [own], [((block, cut * own_cols), bf16)] * 2, []
    )
    halves, places = [[h] for h in halves], [[0], [0]]
    steps, downs, sources = steps_of(n_row), steps_of(n_vec)[:0:-1], [n_vec - 1]
    for i in range(max(len(steps), len(downs))):
        if i < len(steps):
            for which, step in enumerate((steps[-1 - i], steps[i])):
                known = jnp.concatenate(halves[which], axis=0)
                halves[which] = [known, swapped(known, ROW, step)]
                places[which] = places[which] + [q ^ step for q in places[which]]
        if i < len(downs):
            part += lax.ppermute(part, VEC, [(v, v ^ downs[i]) for v in sources])
            sources += [v ^ downs[i] for v in sources]
        if i == 0:
            halves, part, other_cols = lax.optimization_barrier((halves, part, other_cols))

    pieces = [part]
    for q in range(1, n_row):
        to = 0 if q < n_row // 2 else 1
        pairs = [(r * n_vec + i, (r ^ q) * n_vec + (i ^ to)) for r in range(n_row) for i in holders]
        pieces.append(lax.ppermute(part, (ROW, VEC), pairs))
    count = n_vec * own_cols // 2
    parts = sum(halves, [])
    rotated, peak = call(
        functools.partial(rotate_kernel, places), flags, [filtered, shared, *parts],
        [((2 * rows, count), f32), ((8, count), f32)], [], 1 << 31,
    )
    pieces, rotated, peak = lax.optimization_barrier((pieces, rotated, peak))
    here = jnp.concatenate([pieces[q] + pieces[q + n_row // 2] for q in range(n_row // 2)], axis=0)
    tails = [here, swapped(here, VEC, 1)]

    def finish(which):
        return call(
            functools.partial(finish_kernel, places[which], depth, which), flags,
            [panel_inverse, *tails, *halves[which], rotated, peak, cols, other_cols],
            [((2 * rows, count // 2), f32), ((8, count // 2), f32)],
            [
                pltpu.VMEM((4 * width, count // 2), bf16), pltpu.VMEM(cross.shape, bf16),
                pltpu.VMEM((2 * width, count // 2), f32),
            ],
        )

    piece = lambda values, i: values[:, i * own_cols : (i + 1) * own_cols]
    values, _ = finish(0)
    values = [piece(values, j).astype(jnp.float16) for j in range(cut)]
    values, panel_inverse = lax.optimization_barrier((values, panel_inverse))
    far = {2 * (cut + j): [swapped(values[j], VEC, 2 * (cut + j))] for j in range(cut)}
    values, power = finish(1)
    near = {}
    for j in range(1, cut):
        value = piece(values, j).astype(jnp.float16)
        near[2 * j] = [swapped(v, VEC, 2 * j) for v in (value[:rows], value[rows:])]
    near[0] = [piece(values, 0)]

    shape = jax.ShapeDtypeStruct((n_vec * rows, own_cols), f32)
    spec = lambda space: pl.BlockSpec(memory_space=space)

    def place(blocks, out):
        parts = sum(blocks.values(), [])
        return pl.pallas_call(
            functools.partial(place_kernel, [(k, len(v)) for k, v in blocks.items()]),
            in_specs=[spec(pltpu.SMEM)] + [spec(pltpu.VMEM)] * (1 + len(parts)) + [spec(pl.ANY)] * len(out),
            out_specs=spec(pl.ANY), out_shape=shape,
            scratch_shapes=[
                pltpu.VMEM((len(blocks), 2 * rows, own_cols), f32), pltpu.SemaphoreType.DMA((len(blocks),))
            ],
            input_output_aliases={2 + len(parts): 0} if out else {},
            compiler_params=pltpu.CompilerParams(vmem_limit_bytes=VMEM_LIMIT),
            cost_estimate=pl.CostEstimate(flops=1, bytes_accessed=1, transcendentals=0),
        )(flags, power, *(v.astype(f32) for v in parts), *out)

    last_far = max(far)
    near.update({k: v for k, v in far.items() if k != last_far})
    return place({last_far: far[last_far]}, [place(near, [])])


def solution(mesh):
    in_specs = (P((ROW, VEC), None), P(ROW, VEC), P((ROW, VEC), None), P())
    return jax.shard_map(on_device, mesh=mesh, in_specs=in_specs, out_specs=P(ROW, VEC), check_vma=False)
```

```python
import functools

import jax
import jax.numpy as jnp
from jax import lax
from jax.experimental import pallas as pl
from jax.experimental.pallas import tpu as pltpu
from jax.sharding import PartitionSpec as P

ROW, VEC = "row", "vec"
VMEM_LIMIT = 16 * 1024 * 1024


def swapped(value, axis, offset):
    return lax.ppermute(value, axis, [(i, i ^ offset) for i in range(lax.axis_size(axis))])


def steps_of(size):
    return [1 << i for i in range(size.bit_length() - 1)]


def split(value):
    high = value.astype(jnp.bfloat16)
    return high, (value - high.astype(jnp.float32)).astype(jnp.bfloat16)


def split_array(value):
    high = lax.reduce_precision(value, 8, 7)
    return high.astype(jnp.bfloat16), (value - high).astype(jnp.bfloat16)


def mul(a, b):
    return jnp.dot(a, b, preferred_element_type=jnp.float32)


def mul3(a, b):
    left = jnp.concatenate([a[0], a[0], a[1]], axis=1)
    return mul(left, jnp.concatenate([b[0], b[1], b[0]], axis=0))


def side_kernel(order, parts, first, second):
    cut, width = len(order) // 2, parts.shape[2]
    for i, j in enumerate(order):
        (first, second)[i // cut][:, i % cut * width : (i % cut + 1) * width] = parts[j]


def gathered(parts, places, block):
    each = parts[0].shape[0] // block
    where = {q: (parts[j // each], j % each) for j, q in enumerate(places)}
    return jnp.concatenate([p[i * block : (i + 1) * block, :] for p, i in (where[q] for q in sorted(where))], axis=0)


def rotate_kernel(places, flags, own, other, *refs):
    *parts, out, peak = refs
    n_row, each, rows = len(places[0]), len(parts) // 2, own.shape[0]
    block = own.shape[1] // n_row
    for i, order in enumerate(places):
        ritz = gathered(parts[i * each : (i + 1) * each], order, block)
        where = slice(i * ritz.shape[1], (i + 1) * ritz.shape[1])
        for filtered, core in ((own, flags[1]), (other, 1 - flags[1])):
            left = jnp.concatenate(
                [filtered[:, pl.ds(pl.multiple_of((flags[2] ^ q) * block, block), block)] for q in range(n_row)], axis=1
            )
            out[pl.ds(pl.multiple_of(core * rows, rows), rows), where] = mul(left, ritz)
        most = jnp.max(jnp.abs(ritz.astype(jnp.float32)), axis=0, keepdims=True)
        peak[:, where] = jnp.broadcast_to(most, (peak.shape[0], most.shape[1]))


def solve_kernel(places, flags, inverse, *refs):
    n_row = len(places)
    here, there, parts, (out, cross, solved) = refs[0], refs[1], refs[2:-3], refs[-3:]
    size = 2 * here.shape[0] // n_row
    width = inverse.shape[1]
    block = here.shape[1]
    cross_rows = cross.shape[0] // n_row

    def tail(sent):
        rows = jnp.concatenate([t[start : start + 2 * width, :] for t, start in sent], axis=1)
        for q in range(n_row):
            start = pl.multiple_of((flags[2] ^ q) * cross_rows, cross_rows)
            t, first = sent[q]
            cross[pl.ds(start, cross_rows), :] = t[first + 2 * width : first + size, :]
        solved[...] = mul(rows, gathered(parts, places, block))

    def pieces(first, second):
        return [((first, second)[2 * q // n_row], q % (n_row // 2) * size) for q in range(n_row)]

    pl.when(flags[1] == 1)(lambda: tail(pieces(here, there)))
    pl.when(flags[1] == 0)(lambda: tail(pieces(there, here)))
    if block == 2 * width:
        between = cross[:, :width], cross[:, width:]
    else:
        between = cross[:width, :], cross[width:, :]
    last = mul3(split(inverse[1]), split(solved[width:, :]))
    middle = solved[:width, :] - mul3(between, split(last))
    after = mul3(split(inverse[0]), split(middle))
    out[width : 2 * width, :], out[3 * width :, :] = split(last)
    out[:width, :], out[2 * width : 3 * width, :] = split(after)


def correct_kernel(depth, which, flags, rotated, peak, own, other, solved, out, power):
    rows, size = own.shape[0], own.shape[1] // 2
    half = out.shape[1]
    where = slice(which * half, (which + 1) * half)
    panels = solved[:size, :].astype(jnp.float32) + solved[size:, :].astype(jnp.float32)
    bound = 8.0 * depth * peak[0:1, where] + size * jnp.max(jnp.abs(panels), axis=0, keepdims=True)
    exponent = 14.0 - jnp.floor(jnp.log2(jnp.maximum(bound, 1e-30)))
    scale = jnp.exp2(exponent)
    power[...] = jnp.broadcast_to(jnp.exp2(-exponent), power.shape)
    right = jnp.concatenate([solved[...], solved[:size, :]], axis=0)
    for cols, core in ((own, flags[1]), (other, 1 - flags[1])):
        at = pl.ds(pl.multiple_of(core * rows, rows), rows)
        left = jnp.concatenate([cols[:, :size], cols[...]], axis=1)
        out[at, :] = (rotated[at, where] - mul(left, right)) * scale

    @pl.when(flags[0] == 1)
    def _():
        out[2 * rows - size :, :] = panels * scale


def finish_kernel(places, depth, which, flags, inverse, here, there, *refs):
    *parts, rotated, peak, own, other, out, power, terms, cross, solved = refs
    solve_kernel(places, flags, inverse, here, there, *parts, terms, cross, solved)
    correct_kernel(depth, which, flags, rotated, peak, own, other, terms, out, power)


def place_kernel(ks, flags, power, *refs):
    out, ready, sems = refs[-3:]
    size, width = ready.shape[1:]
    parts = list(refs)
    copies = []
    for i, (k, count) in enumerate(ks):
        for j in range(count):
            part = parts.pop(0)
            step = size // 4
            for start in range(0, part.shape[0], step):
                at = j * part.shape[0] + start
                ready[i, at : at + step, :] = part[start : start + step, :] * power[0:1, :width]
                into = out.at[pl.ds(pl.multiple_of(((flags[3] ^ k) >> 1) * size + at, step), step), :]
                copies.append(pltpu.make_async_copy(ready.at[i, pl.ds(at, step), :], into, sems.at[len(copies)]))
                copies[-1].start()
    for copy in copies:
        copy.wait()


def call(kernel, flags, inputs, out_shape, scratch, work=1):
    spec = lambda space: pl.BlockSpec(memory_space=space)
    specs, arrays, scalars = [], [], [] if flags is None else [flags]
    for value in inputs:
        group = value if isinstance(value, list) else [value]
        specs += [spec(pltpu.HBM if isinstance(value, list) else pltpu.VMEM)] * len(group)
        arrays += group
    return pl.pallas_call(
        kernel,
        in_specs=[spec(pltpu.SMEM)] * len(scalars) + specs,
        out_specs=[spec(pltpu.VMEM)] * len(out_shape),
        out_shape=[jax.ShapeDtypeStruct(*s) for s in out_shape],
        scratch_shapes=scratch,
        compiler_params=pltpu.CompilerParams(vmem_limit_bytes=VMEM_LIMIT),
        cost_estimate=pl.CostEstimate(flops=work, bytes_accessed=1, transcendentals=0),
    )(*scalars, *arrays)


def on_device(filtered, ritz, panel_cols, panel_inverse):
    rows, depth = filtered.shape
    width = panel_inverse.shape[1]
    n_row, n_vec = lax.axis_size(ROW), lax.axis_size(VEC)
    row, vec = lax.axis_index(ROW), lax.axis_index(VEC)
    block, own_cols = ritz.shape
    is_last = (row == n_row - 1) & (vec == n_vec - 1)
    last = n_row * n_vec - 1
    lower = rows - 2 * width
    cut = n_vec // 4
    f32, bf16 = jnp.float32, jnp.bfloat16
    holders = range(1, n_vec, 2)

    last_chip = (row == n_row - 1) & (vec >= n_vec - 2)
    flags = jnp.stack([last_chip.astype(jnp.int32), vec & 1, row, vec])
    filtered, ritz, panel_cols, flags, is_last = lax.optimization_barrier((filtered, ritz, panel_cols, flags, is_last))

    cross = jnp.concatenate(split_array(panel_cols[lower : lower + width, width:]), axis=1 if block == 2 * width else 0)
    cross_rows = cross.shape[0] // n_row
    def part_of(r):
        return jnp.concatenate(
            [filtered[lower:, r * block : (r + 1) * block], cross[r * cross_rows : (r + 1) * cross_rows]], axis=0
        )
    own, evens = ritz[None], [0]
    for step in steps_of(n_vec)[:0:-1]:
        own = jnp.concatenate([own, swapped(own, VEC, step)])
        evens += [k ^ step for k in evens]
    shared = swapped(filtered, VEC, 1)
    parts = [lax.ppermute(part_of(r), (ROW, VEC), [(last, r * n_vec + n_vec - 1)]) for r in range(n_row - 1)]
    part = sum(parts, jnp.where(is_last, part_of(n_row - 1), jnp.zeros((), bf16)))
    cols = jnp.concatenate(split_array(panel_cols), axis=1)
    own, part, shared, cols = lax.optimization_barrier((own, part, shared, cols))
    other_cols = swapped(cols, VEC, 1)

    order = [evens.index(2 * ((cut + i) % (2 * cut))) for i in range(2 * cut)]
    halves = call(
        functools.partial(side_kernel, order), None, [own], [((block, cut * own_cols), bf16)] * 2, []
    )
    halves, places = [[h] for h in halves], [[0], [0]]
    steps, downs, sources = steps_of(n_row), steps_of(n_vec)[:0:-1], [n_vec - 1]
    for i in range(max(len(steps), len(downs))):
        if i < len(steps):
            for which, step in enumerate((steps[-1 - i], steps[i])):
                known = jnp.concatenate(halves[which], axis=0)
                halves[which] = [known, swapped(known, ROW, step)]
                places[which] = places[which] + [q ^ step for q in places[which]]
        if i < len(downs):
            part += lax.ppermute(part, VEC, [(v, v ^ downs[i]) for v in sources])
            sources += [v ^ downs[i] for v in sources]
        if i == 0:
            halves, part, other_cols = lax.optimization_barrier((halves, part, other_cols))

    pieces = [part]
    for q in range(1, n_row):
        to = 0 if q < n_row // 2 else 1
        pairs = [(r * n_vec + i, (r ^ q) * n_vec + (i ^ to)) for r in range(n_row) for i in holders]
        pieces.append(lax.ppermute(part, (ROW, VEC), pairs))
    count = n_vec * own_cols // 2
    parts = sum(halves, [])
    rotated, peak = call(
        functools.partial(rotate_kernel, places), flags, [filtered, shared, *parts],
        [((2 * rows, count), f32), ((8, count), f32)], [], 1 << 31,
    )
    pieces, rotated, peak = lax.optimization_barrier((pieces, rotated, peak))
    here = jnp.concatenate([pieces[q] + pieces[q + n_row // 2] for q in range(n_row // 2)], axis=0)
    tails = [here, swapped(here, VEC, 1)]

    def finish(which):
        return call(
            functools.partial(finish_kernel, places[which], depth, which), flags,
            [panel_inverse, *tails, *halves[which], rotated, peak, cols, other_cols],
            [((2 * rows, count // 2), f32), ((8, count // 2), f32)],
            [
                pltpu.VMEM((4 * width, count // 2), bf16), pltpu.VMEM(cross.shape, bf16),
                pltpu.VMEM((2 * width, count // 2), f32),
            ],
        )

    piece = lambda values, i: values[:, i * own_cols : (i + 1) * own_cols]
    values, _ = finish(0)
    values = [piece(values, j).astype(jnp.float16) for j in range(cut)]
    values, panel_inverse = lax.optimization_barrier((values, panel_inverse))
    far = {2 * (cut + j): [swapped(values[j], VEC, 2 * (cut + j))] for j in range(cut)}
    values, power = finish(1)
    near = {}
    for j in range(1, cut):
        value = piece(values, j).astype(jnp.float16)
        near[2 * j] = [swapped(v, VEC, 2 * j) for v in (value[:rows], value[rows:])]
    near[0] = [piece(values, 0)]

    shape = jax.ShapeDtypeStruct((n_vec * rows, own_cols), f32)
    spec = lambda space: pl.BlockSpec(memory_space=space)

    def place(blocks, out):
        parts = sum(blocks.values(), [])
        return pl.pallas_call(
            functools.partial(place_kernel, [(k, len(v)) for k, v in blocks.items()]),
            in_specs=[spec(pltpu.SMEM)] + [spec(pltpu.VMEM)] * (1 + len(parts)) + [spec(pl.ANY)] * len(out),
            out_specs=spec(pl.ANY), out_shape=shape,
            scratch_shapes=[
                pltpu.VMEM((len(blocks), 2 * rows, own_cols), f32), pltpu.SemaphoreType.DMA((4 * len(blocks),))
            ],
            input_output_aliases={2 + len(parts): 0} if out else {},
            compiler_params=pltpu.CompilerParams(vmem_limit_bytes=VMEM_LIMIT),
            cost_estimate=pl.CostEstimate(flops=1, bytes_accessed=1, transcendentals=0),
        )(flags, power, *(v.astype(f32) for v in parts), *out)

    last_far = max(far)
    near.update({k: v for k, v in far.items() if k != last_far})
    return place({last_far: far[last_far]}, [place(near, [])])


def solution(mesh):
    in_specs = (P((ROW, VEC), None), P(ROW, VEC), P((ROW, VEC), None), P())
    return jax.shard_map(on_device, mesh=mesh, in_specs=in_specs, out_specs=P(ROW, VEC), check_vma=False)
```

```python
import functools

import jax
import jax.numpy as jnp
from jax import lax
from jax.experimental import pallas as pl
from jax.experimental.pallas import tpu as pltpu
from jax.sharding import PartitionSpec as P

ROW, VEC = "row", "vec"
VMEM_LIMIT = 16 * 1024 * 1024


def swapped(value, axis, offset):
    return lax.ppermute(value, axis, [(i, i ^ offset) for i in range(lax.axis_size(axis))])


def steps_of(size):
    return [1 << i for i in range(size.bit_length() - 1)]


def split(value):
    high = value.astype(jnp.bfloat16)
    return high, (value - high.astype(jnp.float32)).astype(jnp.bfloat16)


def split_array(value):
    high = lax.reduce_precision(value, 8, 7)
    return high.astype(jnp.bfloat16), (value - high).astype(jnp.bfloat16)


def mul(a, b):
    return jnp.dot(a, b, preferred_element_type=jnp.float32)


def mul3(a, b):
    left = jnp.concatenate([a[0], a[0], a[1]], axis=1)
    return mul(left, jnp.concatenate([b[0], b[1], b[0]], axis=0))


def side_kernel(order, parts, first, second):
    cut, width = len(order) // 2, parts.shape[2]
    for i, j in enumerate(order):
        (first, second)[i // cut][:, i % cut * width : (i % cut + 1) * width] = parts[j]


def gathered(parts, places, block):
    each = parts[0].shape[0] // block
    where = {q: (parts[j // each], j % each) for j, q in enumerate(places)}
    return jnp.concatenate([p[i * block : (i + 1) * block, :] for p, i in (where[q] for q in sorted(where))], axis=0)


def rotate_kernel(places, flags, own, other, *refs):
    *parts, out, peak = refs
    n_row, each, rows = len(places[0]), len(parts) // 2, own.shape[0]
    block = own.shape[1] // n_row
    for i, order in enumerate(places):
        ritz = gathered(parts[i * each : (i + 1) * each], order, block)
        where = slice(i * ritz.shape[1], (i + 1) * ritz.shape[1])
        for filtered, core in ((own, flags[1]), (other, 1 - flags[1])):
            left = jnp.concatenate(
                [filtered[:, pl.ds(pl.multiple_of((flags[2] ^ q) * block, block), block)] for q in range(n_row)], axis=1
            )
            out[pl.ds(pl.multiple_of(core * rows, rows), rows), where] = mul(left, ritz)
        most = jnp.max(jnp.abs(ritz.astype(jnp.float32)), axis=0, keepdims=True)
        peak[:, where] = jnp.broadcast_to(most, (peak.shape[0], most.shape[1]))


def solve_kernel(places, flags, inverse, *refs):
    n_row = len(places)
    here, there, parts, (out, cross, solved) = refs[0], refs[1], refs[2:-3], refs[-3:]
    size = 2 * here.shape[0] // n_row
    width = inverse.shape[1]
    block = here.shape[1]
    cross_rows = cross.shape[0] // n_row

    def tail(sent):
        rows = jnp.concatenate([t[start : start + 2 * width, :] for t, start in sent], axis=1)
        for q in range(n_row):
            start = pl.multiple_of((flags[2] ^ q) * cross_rows, cross_rows)
            t, first = sent[q]
            cross[pl.ds(start, cross_rows), :] = t[first + 2 * width : first + size, :]
        solved[...] = mul(rows, gathered(parts, places, block))

    def pieces(first, second):
        return [((first, second)[2 * q // n_row], q % (n_row // 2) * size) for q in range(n_row)]

    pl.when(flags[1] == 1)(lambda: tail(pieces(here, there)))
    pl.when(flags[1] == 0)(lambda: tail(pieces(there, here)))
    if block == 2 * width:
        between = cross[:, :width], cross[:, width:]
    else:
        between = cross[:width, :], cross[width:, :]
    last = mul3(split(inverse[1]), split(solved[width:, :]))
    middle = solved[:width, :] - mul3(between, split(last))
    after = mul3(split(inverse[0]), split(middle))
    out[width : 2 * width, :], out[3 * width :, :] = split(last)
    out[:width, :], out[2 * width : 3 * width, :] = split(after)


def correct_kernel(depth, which, flags, rotated, peak, own, other, solved, out, power):
    rows, size = own.shape[0], own.shape[1] // 2
    half = out.shape[1]
    where = slice(which * half, (which + 1) * half)
    panels = solved[:size, :].astype(jnp.float32) + solved[size:, :].astype(jnp.float32)
    bound = 8.0 * depth * peak[0:1, where] + size * jnp.max(jnp.abs(panels), axis=0, keepdims=True)
    exponent = 14.0 - jnp.floor(jnp.log2(jnp.maximum(bound, 1e-30)))
    scale = jnp.exp2(exponent)
    power[...] = jnp.broadcast_to(jnp.exp2(-exponent), power.shape)
    twice = jnp.concatenate([solved[:size, :], solved[:size, :]], axis=0)
    for cols, core in ((own, flags[1]), (other, 1 - flags[1])):
        at = pl.ds(pl.multiple_of(core * rows, rows), rows)
        total = mul(cols[...], twice) + mul(cols[:, :size], solved[size:, :])
        out[at, :] = (rotated[at, where] - total) * scale

    @pl.when(flags[0] == 1)
    def _():
        out[2 * rows - size :, :] = panels * scale


def finish_kernel(places, depth, which, flags, inverse, here, there, *refs):
    *parts, rotated, peak, own, other, out, power, terms, cross, solved = refs
    solve_kernel(places, flags, inverse, here, there, *parts, terms, cross, solved)
    correct_kernel(depth, which, flags, rotated, peak, own, other, terms, out, power)


def place_kernel(ks, flags, power, *refs):
    out, ready, sems = refs[-3:]
    size, width = ready.shape[1:]
    parts = list(refs)
    copies = []
    for i, (k, count) in enumerate(ks):
        for j in range(count):
            part = parts.pop(0)
            step = size // 4
            for start in range(0, part.shape[0], step):
                at = j * part.shape[0] + start
                ready[i, at : at + step, :] = part[start : start + step, :] * power[0:1, :width]
                into = out.at[pl.ds(pl.multiple_of(((flags[3] ^ k) >> 1) * size + at, step), step), :]
                copies.append(pltpu.make_async_copy(ready.at[i, pl.ds(at, step), :], into, sems.at[len(copies)]))
                copies[-1].start()
    for copy in copies:
        copy.wait()


def call(kernel, flags, inputs, out_shape, scratch, work=1):
    spec = lambda space: pl.BlockSpec(memory_space=space)
    specs, arrays, scalars = [], [], [] if flags is None else [flags]
    for value in inputs:
        group = value if isinstance(value, list) else [value]
        specs += [spec(pltpu.HBM if isinstance(value, list) else pltpu.VMEM)] * len(group)
        arrays += group
    return pl.pallas_call(
        kernel,
        in_specs=[spec(pltpu.SMEM)] * len(scalars) + specs,
        out_specs=[spec(pltpu.VMEM)] * len(out_shape),
        out_shape=[jax.ShapeDtypeStruct(*s) for s in out_shape],
        scratch_shapes=scratch,
        compiler_params=pltpu.CompilerParams(vmem_limit_bytes=VMEM_LIMIT),
        cost_estimate=pl.CostEstimate(flops=work, bytes_accessed=1, transcendentals=0),
    )(*scalars, *arrays)


def on_device(filtered, ritz, panel_cols, panel_inverse):
    rows, depth = filtered.shape
    width = panel_inverse.shape[1]
    n_row, n_vec = lax.axis_size(ROW), lax.axis_size(VEC)
    row, vec = lax.axis_index(ROW), lax.axis_index(VEC)
    block, own_cols = ritz.shape
    is_last = (row == n_row - 1) & (vec == n_vec - 1)
    last = n_row * n_vec - 1
    lower = rows - 2 * width
    cut = n_vec // 4
    f32, bf16 = jnp.float32, jnp.bfloat16
    holders = range(1, n_vec, 2)

    last_chip = (row == n_row - 1) & (vec >= n_vec - 2)
    flags = jnp.stack([last_chip.astype(jnp.int32), vec & 1, row, vec])
    filtered, ritz, panel_cols, flags, is_last = lax.optimization_barrier((filtered, ritz, panel_cols, flags, is_last))

    cross = jnp.concatenate(split_array(panel_cols[lower : lower + width, width:]), axis=1 if block == 2 * width else 0)
    cross_rows = cross.shape[0] // n_row
    def part_of(r):
        return jnp.concatenate(
            [filtered[lower:, r * block : (r + 1) * block], cross[r * cross_rows : (r + 1) * cross_rows]], axis=0
        )
    own, evens = ritz[None], [0]
    for step in steps_of(n_vec)[:0:-1]:
        own = jnp.concatenate([own, swapped(own, VEC, step)])
        evens += [k ^ step for k in evens]
    shared = swapped(filtered, VEC, 1)
    parts = [lax.ppermute(part_of(r), (ROW, VEC), [(last, r * n_vec + n_vec - 1)]) for r in range(n_row - 1)]
    part = sum(parts, jnp.where(is_last, part_of(n_row - 1), jnp.zeros((), bf16)))
    cols = jnp.concatenate(split_array(panel_cols), axis=1)
    own, part, shared, cols = lax.optimization_barrier((own, part, shared, cols))
    other_cols = swapped(cols, VEC, 1)

    order = [evens.index(2 * ((cut + i) % (2 * cut))) for i in range(2 * cut)]
    halves = call(
        functools.partial(side_kernel, order), None, [own], [((block, cut * own_cols), bf16)] * 2, []
    )
    halves, places = [[h] for h in halves], [[0], [0]]
    steps, downs, sources = steps_of(n_row), steps_of(n_vec)[:0:-1], [n_vec - 1]
    for i in range(max(len(steps), len(downs))):
        if i < len(steps):
            for which, step in enumerate((steps[-1 - i], steps[i])):
                known = jnp.concatenate(halves[which], axis=0)
                halves[which] = [known, swapped(known, ROW, step)]
                places[which] = places[which] + [q ^ step for q in places[which]]
        if i < len(downs):
            part += lax.ppermute(part, VEC, [(v, v ^ downs[i]) for v in sources])
            sources += [v ^ downs[i] for v in sources]
        if i == 0:
            halves, part, other_cols = lax.optimization_barrier((halves, part, other_cols))

    pieces = [part]
    for q in range(1, n_row):
        to = 0 if q < n_row // 2 else 1
        pairs = [(r * n_vec + i, (r ^ q) * n_vec + (i ^ to)) for r in range(n_row) for i in holders]
        pieces.append(lax.ppermute(part, (ROW, VEC), pairs))
    count = n_vec * own_cols // 2
    parts = sum(halves, [])
    rotated, peak = call(
        functools.partial(rotate_kernel, places), flags, [filtered, shared, *parts],
        [((2 * rows, count), f32), ((8, count), f32)], [], 1 << 31,
    )
    pieces, rotated, peak = lax.optimization_barrier((pieces, rotated, peak))
    here = jnp.concatenate([pieces[q] + pieces[q + n_row // 2] for q in range(n_row // 2)], axis=0)
    tails = [here, swapped(here, VEC, 1)]

    def finish(which):
        return call(
            functools.partial(finish_kernel, places[which], depth, which), flags,
            [panel_inverse, *tails, *halves[which], rotated, peak, cols, other_cols],
            [((2 * rows, count // 2), f32), ((8, count // 2), f32)],
            [
                pltpu.VMEM((4 * width, count // 2), bf16), pltpu.VMEM(cross.shape, bf16),
                pltpu.VMEM((2 * width, count // 2), f32),
            ],
        )

    piece = lambda values, i: values[:, i * own_cols : (i + 1) * own_cols]
    values, _ = finish(0)
    values = [piece(values, j).astype(jnp.float16) for j in range(cut)]
    values, panel_inverse = lax.optimization_barrier((values, panel_inverse))
    far = {2 * (cut + j): [swapped(values[j], VEC, 2 * (cut + j))] for j in range(cut)}
    values, power = finish(1)
    near = {}
    for j in range(1, cut):
        value = piece(values, j).astype(jnp.float16)
        near[2 * j] = [swapped(v, VEC, 2 * j) for v in (value[:rows], value[rows:])]
    near[0] = [piece(values, 0)]

    shape = jax.ShapeDtypeStruct((n_vec * rows, own_cols), f32)
    spec = lambda space: pl.BlockSpec(memory_space=space)

    def place(blocks, out):
        parts = sum(blocks.values(), [])
        return pl.pallas_call(
            functools.partial(place_kernel, [(k, len(v)) for k, v in blocks.items()]),
            in_specs=[spec(pltpu.SMEM)] + [spec(pltpu.VMEM)] * (1 + len(parts)) + [spec(pl.ANY)] * len(out),
            out_specs=spec(pl.ANY), out_shape=shape,
            scratch_shapes=[
                pltpu.VMEM((len(blocks), 2 * rows, own_cols), f32), pltpu.SemaphoreType.DMA((4 * len(blocks),))
            ],
            input_output_aliases={2 + len(parts): 0} if out else {},
            compiler_params=pltpu.CompilerParams(vmem_limit_bytes=VMEM_LIMIT),
            cost_estimate=pl.CostEstimate(flops=1, bytes_accessed=1, transcendentals=0),
        )(flags, power, *(v.astype(f32) for v in parts), *out)

    last_far = max(far)
    near.update({k: v for k, v in far.items() if k != last_far})
    return place({last_far: far[last_far]}, [place(near, [])])


def solution(mesh):
    in_specs = (P((ROW, VEC), None), P(ROW, VEC), P((ROW, VEC), None), P())
    return jax.shard_map(on_device, mesh=mesh, in_specs=in_specs, out_specs=P(ROW, VEC), check_vma=False)
```
